32 devices in a mesh: tile: 8 (over y, x, core), freq: 4 (over z).
Axes of the slice: x: 2, y: 2, z: 4, core: 2. Of those that a mesh axis runs over, the one named last changes fastest.
Arguments:
- data_spectrum: float32 [2, 32, 512, 1024], P(None, 'freq', 'tile'), may hold values from -24 to 24
- velocity_level: int32 [512, 1024], P('tile'), may hold values from 0 to 11
Outputs:
- primaries: float32 [64, 512, 1024], P(None, 'tile', 'freq')
- multiples: float32 [64, 512, 1024], P(None, 'tile', 'freq')
The draws below stay inside these ranges and needn't reach their ends.
All inputs are finite; a program needn't handle non-finite values.
Results may differ from the reference program's by a relative error of at most 0.0003.
Values sent between devices are 32-bit elements; how exact they have to be, the bound alone decides.
A program may use at most 128 MiB of HBM per device.

```python
import math
import jax
import jax.numpy as jnp
from jax import lax

CX = 64
NY = 1024
FREQS = 32
LEVELS = 12
GROUPS = 3
PASSES = 3
NX = 512
SAMPLES = 64


def draw_data_spectrum(key, part):
    noise_key = jax.random.fold_in(key, 11)
    scale_key = jax.random.fold_in(key, 23)
    full_shape = (2, FREQS, NX, NY)
    log_scale = jax.random.uniform(scale_key, (NX, NY), jnp.float32, math.log(0.4), math.log(4.0))
    noise = jnp.clip(jax.random.normal(noise_key, full_shape, jnp.float32), -6.0, 6.0)
    return (noise * jnp.exp(log_scale)).astype(jnp.float32)


def with_ends(result, key, low, top_value):
    shape = result.shape
    spot = [jax.random.randint(jax.random.fold_in(key, axis), (), 0, shape[axis]) for axis in range(len(shape))]
    result = result.at[tuple(spot)].set(low)
    longest = shape.index(max(shape))
    spot[longest] = (spot[longest] + 1) % shape[longest]
    return result.at[tuple(spot)].set(top_value)


def setup_inputs(seed: int = 0) -> dict:
    key_of = jax.random.split(jax.random.key(seed), 3)
    data_spectrum = draw_data_spectrum(jax.random.fold_in(key_of[2], 71), 0)
    velocity_level = with_ends(jax.random.randint(key_of[1], (NX, NY), 0, LEVELS), jax.random.fold_in(key_of[1], 1), 0, LEVELS - 1).astype(jnp.int32)
    return dict(data_spectrum=data_spectrum, velocity_level=velocity_level)


damping = 0.2
paraxial_top = 0.1
depth_step = 10.0
cell_width = 12.5
step_size = 0.6
energy_floor = 1e-05
filter_reach = 2

def coefficients(levels, angular):
    velocity = 1500.0 + 250.0 * levels.astype(jnp.float32)
    phase_angle = angular * depth_step / velocity
    freq_ratio = velocity / (angular * cell_width)
    return (jnp.cos(phase_angle), jnp.sin(phase_angle), paraxial_top * freq_ratio / (1.0 + freq_ratio))

def advance(padded, phase_cos, phase_sin, paraxial):
    centre = padded[..., 1:-1, :]
    pad_widths = [(0, 0)] * (centre.ndim - 1) + [(1, 1)]
    beside = jnp.pad(centre, pad_widths)
    laplace = padded[..., 2:, :] + padded[..., :-2, :] + beside[..., 2:] + beside[..., :-2] - 4.0 * centre
    real_part = centre[0] + damping * laplace[0] - paraxial * laplace[1]
    imag_part = centre[1] + damping * laplace[1] + paraxial * laplace[0]
    return jnp.stack([phase_cos * real_part - phase_sin * imag_part, phase_sin * real_part + phase_cos * imag_part])

def trace_basis(orders):
    samples = 2 * orders
    sample_times = jnp.arange(samples, dtype=jnp.float32)[:, None] + 0.5
    numbers = jnp.arange(orders, dtype=jnp.float32)[None, :] + 1.0
    angles = 2.0 * math.pi * numbers * sample_times / samples
    norming = 1.0 / math.sqrt(orders)
    return jnp.concatenate([jnp.cos(angles), -jnp.sin(angles)], axis=1) * norming

def to_traces(spectrum):
    orders = spectrum.shape[1]
    stacked = spectrum.reshape(2 * orders, spectrum.shape[2] * spectrum.shape[3])
    traces = jnp.dot(trace_basis(orders), stacked, precision=lax.Precision.HIGHEST, preferred_element_type=jnp.float32)
    return traces.reshape(2 * orders, spectrum.shape[2], spectrum.shape[3])

def combine_taps(weights, neighbours):
    filtered = weights[0][None] * neighbours[0]
    for weight, neighbour in zip(weights[1:], neighbours[1:]):
        filtered = filtered + weight[None] * neighbour
    return filtered

def subtract(recorded, padded):
    row_count = recorded.shape[1]
    col_count = recorded.shape[2]
    diameter = 2 * filter_reach + 1
    neighbours = [padded[:, row_off:row_off + row_count, col_off:col_off + col_count] for row_off in range(diameter) for col_off in range(diameter)]
    trace_power = lax.optimization_barrier(jnp.sum(padded * padded, axis=0))
    energy = energy_floor + trace_power[0:row_count, 0:col_count]
    for row_off in range(diameter):
        for col_off in range(diameter):
            if row_off + col_off > 0:
                energy = energy + trace_power[row_off:row_off + row_count, col_off:col_off + col_count]
    weights = [jnp.zeros((row_count, col_count), jnp.float32) for neighbour in neighbours]
    for repeat in range(PASSES):
        residual = recorded - combine_taps(weights, neighbours)
        weights = [weight + step_size * lax.optimization_barrier(jnp.sum(residual * neighbour, axis=0)) / energy for weight, neighbour in zip(weights, neighbours)]
    return recorded - combine_taps(weights, neighbours)

def reference(data_spectrum, velocity_level):
    angular = 4.0 * math.pi * (jnp.arange(FREQS, dtype=jnp.float32) + 1.0)

    def extrapolate(inputs):
        spectrum, frequency = inputs
        phase_cos, phase_sin, paraxial = coefficients(velocity_level, frequency)

        def one_step(counter, wavefield):
            padded = jnp.pad(wavefield, ((0, 0), (1, 1), (0, 0)))
            return advance(padded, phase_cos, phase_sin, paraxial)
        return -lax.fori_loop(0, 4 * GROUPS, one_step, spectrum)
    predicted = lax.map(extrapolate, (jnp.moveaxis(data_spectrum, 1, 0), angular))
    multiple_spectrum = jnp.moveaxis(predicted, 0, 1)
    data_traces = to_traces(data_spectrum)
    multiples = to_traces(multiple_spectrum)
    padded = jnp.pad(multiples, ((0, 0), (filter_reach, filter_reach), (filter_reach, filter_reach)))

    def one_block(block_index):
        first_row = (block_index * CX).astype(jnp.int32)
        part_padded = lax.dynamic_slice_in_dim(padded, first_row, CX + 2 * filter_reach, 1)
        part_data = lax.dynamic_slice_in_dim(data_traces, first_row, CX, 1)
        return subtract(part_data, part_padded)
    pieces = lax.map(one_block, jnp.arange(NX // CX, dtype=jnp.int32))
    primaries = jnp.moveaxis(pieces, 0, 1).reshape(SAMPLES, NX, NY)
    return (primaries, multiples)
```

```python
import functools
import math

import jax
import jax.numpy as jnp
import ml_dtypes
import numpy as np
from jax import lax
from jax.experimental import pallas as pl
from jax.experimental.pallas import tpu as pltpu
from jax.sharding import PartitionSpec as P

GROUPS = 3
PASSES = 3
STEPS = 4 * GROUPS

damping = 0.2
paraxial_top = 0.1
depth_step = 10.0
cell_width = 12.5
step_size = 0.6
energy_floor = 1e-05
filter_reach = 2

HALO = 16
LANES = 128
STRIDE = 100
OUTSIDE = 127
MESH = pl.DeviceIdType.MESH


def tile_count(width):
    count = 1
    while STRIDE * count < width + filter_reach + 1:
        count += 1
    return count


def overlapped(pieces, tile, lane):
    origin = STRIDE * tile - HALO + LANES
    k, off = origin // LANES, origin % LANES
    turn = LANES - off
    axis = pieces[0].ndim - 1
    return jnp.where(
        lane < turn, pltpu.roll(pieces[k], turn, axis), pltpu.roll(pieces[k + 1], turn, axis)
    )


def coefficient_table(orders, nz, per_chunk, chunks):
    table = np.zeros((chunks, 4, 8, LANES), np.float64)
    velocity = 1500.0 + 250.0 * np.arange(OUTSIDE)
    for j in range(chunks):
        for s in range(nz):
            for i in range(per_chunk):
                k = s * (orders // nz) + j * per_chunk + i
                omega = 4.0 * math.pi * (k + 1)
                theta = omega * depth_step / velocity
                q = velocity / (omega * cell_width)
                spread = damping + 1j * paraxial_top * q / (1.0 + q)
                turn = np.exp(1j * theta)
                centre = turn * (1.0 - 4.0 * spread)
                beside = turn * spread
                table[j, :, s * per_chunk + i, :OUTSIDE] = np.stack(
                    [centre.real, centre.imag, beside.real, beside.imag]
                )
    return table.astype(np.float32)


def trace_basis(orders, nz, per_chunk, chunks):
    samples = 2 * orders
    times = np.arange(samples)[:, None] + 0.5
    order = [
        s * (orders // nz) + j * per_chunk + i
        for j in range(chunks)
        for s in range(nz)
        for i in range(per_chunk)
    ]
    angles = 2.0 * math.pi * (np.array(order)[None, :] + 1.0) * times / samples
    basis = np.concatenate([np.cos(angles), -np.sin(angles)], axis=1) / math.sqrt(orders)
    basis = basis.astype(np.float32)
    high = basis.astype(ml_dtypes.bfloat16)
    low = (basis - high.astype(np.float32)).astype(ml_dtypes.bfloat16)
    return np.concatenate([high, high, low, low], axis=1)


def predict_kernel(
    tiles, nz, per_chunk, chunks, rows, width,
    x_ref, strip_ref, level_ref, table_ref,
    m_ref, d_ref,
    ext, sext, lext, index, coef, state,
    a_send, a_recv, s_send, s_recv, r_send, r_recv, q_send, q_recv, l_send, l_recv, own,
):
    tile = lax.axis_index("tile")
    me = lax.axis_index("freq")
    has_up = tile > 0
    has_down = tile < tiles - 1
    nt = tile_count(width)
    mains = width // LANES
    full = rows + 2 * HALO
    inner = pl.ds(HALO, rows)
    window = pl.ds(pl.multiple_of(me * width, LANES), width + 2 * LANES)

    barrier = pltpu.get_barrier_semaphore()
    for hop in range(1, nz):
        pl.semaphore_signal(
            barrier, inc=1, device_id=(tile, lax.rem(me + hop, nz)), device_id_type=MESH
        )

    @pl.when(has_up)
    def _():
        pl.semaphore_signal(barrier, inc=1, device_id=(tile - 1, me), device_id_type=MESH)

    @pl.when(has_down)
    def _():
        pl.semaphore_signal(barrier, inc=1, device_id=(tile + 1, me), device_id_type=MESH)

    pl.semaphore_wait(
        barrier, nz - 1 + has_up.astype(jnp.int32) + has_down.astype(jnp.int32)
    )

    def level_copy(up):
        src = level_ref.at[pl.ds(0 if up else rows - HALO, HALO), window]
        dst = lext.at[pl.ds(HALO + rows if up else 0, HALO), :]
        way = 0 if up else 1
        return pltpu.make_async_remote_copy(
            src_ref=src, dst_ref=dst, send_sem=l_send.at[way], recv_sem=l_recv.at[way],
            device_id=(tile + (-1 if up else 1), me), device_id_type=MESH,
        )

    def main_copy(j, dest, source):
        return pltpu.make_async_remote_copy(
            src_ref=x_ref.at[
                :, pl.ds(j * per_chunk, per_chunk), :,
                pl.ds(pl.multiple_of(dest * width, LANES), width),
            ],
            dst_ref=ext.at[j, :, pl.ds(source * per_chunk, per_chunk), inner, :],
            send_sem=a_send.at[j, dest], recv_sem=a_recv.at[j, source],
            device_id=(tile, dest), device_id_type=MESH,
        )

    def strip_copy(j, dest, source):
        return pltpu.make_async_remote_copy(
            src_ref=strip_ref.at[dest, j],
            dst_ref=sext.at[j, source, inner, :],
            send_sem=s_send.at[j, dest], recv_sem=s_recv.at[j, source],
            device_id=(tile, dest), device_id_type=MESH,
        )

    def row_copies(j, up):
        src = pl.ds(HALO if up else rows, HALO)
        dst = pl.ds(HALO + rows if up else 0, HALO)
        way = 0 if up else 1
        target = (tile + (-1 if up else 1), me)
        return (
            pltpu.make_async_remote_copy(
                src_ref=ext.at[j, :, :, src, :], dst_ref=ext.at[j, :, :, dst, :],
                send_sem=r_send.at[j, way], recv_sem=r_recv.at[j, way],
                device_id=target, device_id_type=MESH,
            ),
            pltpu.make_async_remote_copy(
                src_ref=sext.at[j, :, src, :], dst_ref=sext.at[j, :, dst, :],
                send_sem=q_send.at[j, way], recv_sem=q_recv.at[j, way],
                device_id=target, device_id_type=MESH,
            ),
        )

    def own_copies(j):
        return (
            pltpu.make_async_copy(
                x_ref.at[
                    :, pl.ds(j * per_chunk, per_chunk), :,
                    pl.ds(pl.multiple_of(me * width, LANES), width),
                ],
                ext.at[j, :, pl.ds(me * per_chunk, per_chunk), inner, :],
                own.at[j, 0],
            ),
            pltpu.make_async_copy(
                strip_ref.at[me, j], sext.at[j, me, inner, :], own.at[j, 1]
            ),
        )

    own_level = pltpu.make_async_copy(
        level_ref.at[:, window], lext.at[inner, :], own.at[chunks, 0]
    )

    @pl.when(has_up)
    def _():
        level_copy(True).start()

    @pl.when(has_down)
    def _():
        level_copy(False).start()

    own_level.start()

    def send(j, carry):
        for hop in range(1, nz):
            dest = lax.rem(me + hop, nz)
            strip_copy(j, dest, me).start()
            main_copy(j, dest, me).start()
        for copy in own_copies(j):
            copy.start()
        return carry

    lax.fori_loop(0, chunks, send, 0)

    top, bottom = pl.ds(0, HALO), pl.ds(HALO + rows, HALO)
    for missing, edge in ((jnp.logical_not(has_up), top), (jnp.logical_not(has_down), bottom)):

        @pl.when(missing)
        def _(edge=edge):
            lext[edge, :] = jnp.full((HALO, lext.shape[1]), OUTSIDE, jnp.int32)

            def clear(j, carry):
                for part in range(2):
                    for f in range(8):
                        ext[j, part, f, edge, :] = jnp.zeros((HALO, width), jnp.float32)
                for s in range(nz):
                    sext[j, s, edge, :] = jnp.zeros((HALO, LANES), jnp.float32)
                return carry

            lax.fori_loop(0, chunks, clear, 0)

    own_level.wait()

    @pl.when(has_up)
    def _():
        level_copy(True).wait_send()
        level_copy(False).wait_recv()

    @pl.when(has_down)
    def _():
        level_copy(False).wait_send()
        level_copy(True).wait_recv()

    lane2 = lax.broadcasted_iota(jnp.int32, (8, LANES), 1)
    lane3 = lax.broadcasted_iota(jnp.int32, (8, 8, LANES), 2)

    def make_index(b, carry):
        at = pl.ds(pl.multiple_of(b * 8, 8), 8)
        pieces = [lext[at, k * LANES : (k + 1) * LANES] for k in range(mains + 2)]
        for t in range(nt):
            found = overlapped(pieces, t, lane2)
            index[t, at] = jnp.broadcast_to(found[:, None, :], (8, 8, LANES))
        return carry

    lax.fori_loop(0, full // 8, make_index, 0)

    def one_chunk(j, carry):
        for copy in own_copies(j):
            copy.wait()
        for hop in range(1, nz):
            source = lax.rem(me + hop, nz)
            main_copy(j, me, source).wait_recv()
            strip_copy(j, me, source).wait_recv()

        @pl.when(has_up)
        def _():
            for copy in row_copies(j, True):
                copy.start()

        @pl.when(has_down)
        def _():
            for copy in row_copies(j, False):
                copy.start()

        def make_coef(e, carry):
            for t in range(nt):
                at = index[t, e]
                for c in range(4):
                    coef[c, t, e] = jnp.take_along_axis(
                        table_ref[j, c], at, axis=1, mode="promise_in_bounds"
                    )
            return carry

        lax.fori_loop(0, full, make_coef, 0)

        @pl.when(has_up)
        def _():
            for copy in row_copies(j, False):
                copy.wait_recv()

        @pl.when(has_down)
        def _():
            for copy in row_copies(j, True):
                copy.wait_recv()

        def fill(b, carry):
            at = pl.ds(pl.multiple_of(b * 8, 8), 8)
            for part in range(2):
                main = [
                    jnp.swapaxes(ext[j, part, :, at, k * LANES : (k + 1) * LANES], 0, 1)
                    for k in range(mains)
                ]
                strips = []
                for s in range(nz):
                    strip = sext[j, s, at, :]
                    for i in range(per_chunk):
                        base = (part * per_chunk + i) * 2 * HALO
                        strips.append(pltpu.roll(strip, (LANES - base - HALO) % LANES, 1))
                strip = jnp.swapaxes(jnp.stack(strips), 0, 1)
                pieces = [strip] + main + [strip]
                for t in range(nt):
                    state[0, part, t, at] = overlapped(pieces, t, lane3)

                @pl.when((b >= HALO // 8) & (b < (HALO + rows) // 8))
                def _():
                    for k in range(mains):
                        for r in range(8):
                            d_ref[b * 8 - HALO + r, k, part, j] = main[k][r]
            return carry

        lax.fori_loop(0, full // 8, fill, 0)

        def one_step(s, carry):
            old = lax.rem(s + 1, 2)
            new = lax.rem(s, 2)
            first = HALO - filter_reach - STEPS + s
            count = rows + 2 * (filter_reach + STEPS) - 2 * s

            def block(b, carry):
                e = first + 4 * b
                for t in range(nt):
                    re = [state[old, 0, t, e - 1 + r] for r in range(6)]
                    im = [state[old, 1, t, e - 1 + r] for r in range(6)]
                    for r in range(4):
                        a, b_ = re[r + 1], im[r + 1]
                        nr = (re[r] + re[r + 2]) + (
                            pltpu.roll(a, 1, 1) + pltpu.roll(a, LANES - 1, 1)
                        )
                        ni = (im[r] + im[r + 2]) + (
                            pltpu.roll(b_, 1, 1) + pltpu.roll(b_, LANES - 1, 1)
                        )
                        cr, ci = coef[0, t, e + r], coef[1, t, e + r]
                        br, bi = coef[2, t, e + r], coef[3, t, e + r]
                        state[new, 0, t, e + r] = (cr * a - ci * b_) + (br * nr - bi * ni)
                        state[new, 1, t, e + r] = (cr * b_ + ci * a) + (br * ni + bi * nr)
                return carry

            lax.fori_loop(0, (count + 3) // 4, block, 0)
            return carry

        lax.fori_loop(1, STEPS + 1, one_step, 0)

        def put(r, carry):
            for t in range(nt):
                for part in range(2):
                    m_ref[r, t, part, j] = state[STEPS % 2, part, t, r + HALO - filter_reach]
            return carry

        lax.fori_loop(0, rows + 2 * filter_reach, put, 0)
        return carry

    lax.fori_loop(0, chunks, one_chunk, 0)

    def finish(j, carry):
        for hop in range(1, nz):
            dest = lax.rem(me + hop, nz)
            strip_copy(j, dest, me).wait_send()
            main_copy(j, dest, me).wait_send()

        @pl.when(has_up)
        def _():
            for copy in row_copies(j, True):
                copy.wait_send()

        @pl.when(has_down)
        def _():
            for copy in row_copies(j, False):
                copy.wait_send()

        return carry

    lax.fori_loop(0, chunks, finish, 0)


def to_trace(basis, spectrum):
    high = spectrum.astype(jnp.bfloat16)
    low = (spectrum - high.astype(jnp.float32)).astype(jnp.bfloat16)
    both = jnp.concatenate([high, low, high, low], axis=0)
    return jnp.dot(basis, both, preferred_element_type=jnp.float32)


def subtract_kernel(rows, width, m_ref, d_ref, basis_ref, p_ref, q_ref, shifted, data, result):
    i = pl.program_id(0)
    mains = width // LANES
    nt = m_ref.shape[1]
    reach = filter_reach
    diameter = 2 * reach + 1
    samples = basis_ref.shape[0]
    basis = basis_ref[...]
    lane = lax.broadcasted_iota(jnp.int32, (samples, LANES), 1)

    def make_row(r, carry):
        spectrum = jnp.concatenate(
            [m_ref[r, t].reshape(samples, LANES) for t in range(nt)], axis=1
        )
        traces = -to_trace(basis, spectrum)
        for shift in range(diameter):
            for b in range(mains):
                low = LANES * b + shift - reach
                value = None
                for t in range(nt):
                    begin, end = STRIDE * t - reach, STRIDE * (t + 1) - reach
                    if end <= low or begin >= low + LANES:
                        continue
                    tile = traces[:, t * LANES : (t + 1) * LANES]
                    turn = (STRIDE * t - HALO - low) % LANES
                    moved = pltpu.roll(tile, turn, 1) if turn else tile
                    value = moved if value is None else jnp.where(lane < begin - low, value, moved)
                shifted[shift, r, :, b * LANES : (b + 1) * LANES] = value
        return carry

    lax.fori_loop(jnp.where(i == 0, 0, 8 * i + 2 * reach), 8 * i + 8 + 2 * reach, make_row, 0)

    def make_data(r, carry):
        spectrum = jnp.concatenate(
            [d_ref[8 * i + r, b].reshape(samples, LANES) for b in range(mains)], axis=1
        )
        data[r] = to_trace(basis, spectrum)
        return carry

    lax.fori_loop(0, 8, make_data, 0)

    taps = [(a, c) for a in range(diameter) for c in range(diameter)]

    def one_row(n, carry):
        r, b = n // mains, lax.rem(n, mains)
        at = pl.ds(pl.multiple_of(b * LANES, LANES), LANES)

        def tap(a, c):
            return shifted[c, 8 * i + r + a, :, at]

        recorded = data[r, :, at]

        def total(values):
            return jnp.sum(values, axis=0, keepdims=True)

        power = jnp.zeros((8, LANES), jnp.float32)
        for a, c in taps:
            value = tap(a, c)
            power = power + jnp.sum((value * value).reshape(samples // 8, 8, LANES), axis=0)
        gain = step_size / (energy_floor + total(power))
        weights = None
        for repeat in range(PASSES):
            residual = recorded
            if weights is not None:
                for weight, (a, c) in zip(weights, taps):
                    residual = residual - weight * tap(a, c)
            change = [total(residual * tap(a, c)) * gain for a, c in taps]
            weights = (
                change if weights is None else [w + more for w, more in zip(weights, change)]
            )
        residual = recorded
        for weight, (a, c) in zip(weights, taps):
            residual = residual - weight * tap(a, c)
        result[r, :, at] = residual
        return carry

    lax.fori_loop(0, 8 * mains, one_row, 0)

    for k in range(samples // 8):
        part = slice(8 * k, 8 * k + 8)
        p_ref[part] = jnp.swapaxes(result[:, part, :], 0, 1)
        q_ref[part] = jnp.swapaxes(
            shifted[reach, pl.ds(8 * i + reach, 8), part, :], 0, 1
        )


def local(mesh_shape, data_spectrum, velocity_level):
    nz, tiles = mesh_shape["freq"], mesh_shape["tile"]
    _, local_freqs, rows, cols = data_spectrum.shape
    orders = local_freqs * nz
    samples = 2 * orders
    width = cols // nz
    per_chunk = 8 // nz
    chunks = local_freqs // per_chunk
    nt = tile_count(width)
    mains = width // LANES
    full = rows + 2 * HALO
    reach = filter_reach

    around = jnp.pad(data_spectrum, ((0, 0), (0, 0), (0, 0), (HALO, HALO)))
    strips = jnp.stack(
        [
            jnp.concatenate(
                [
                    around[..., d * width : d * width + HALO],
                    around[..., (d + 1) * width + HALO : (d + 1) * width + 2 * HALO],
                ],
                axis=-1,
            )
            for d in range(nz)
        ]
    )
    strips = strips.reshape(nz, 2, chunks, per_chunk, rows, 2 * HALO)
    strips = strips.transpose(0, 2, 4, 1, 3, 5).reshape(nz, chunks, rows, -1)
    strips = jnp.pad(strips, ((0, 0),) * 3 + ((0, LANES - strips.shape[-1]),))
    levels = jnp.pad(velocity_level, ((0, 0), (LANES, LANES)), constant_values=OUTSIDE)
    table = jnp.asarray(coefficient_table(orders, nz, per_chunk, chunks))
    basis = jnp.asarray(trace_basis(orders, nz, per_chunk, chunks))

    dma = pltpu.SemaphoreType.DMA
    vmem = pl.BlockSpec(memory_space=pltpu.VMEM)
    hbm = pl.BlockSpec(memory_space=pl.ANY)
    predicted, recorded = pl.pallas_call(
        functools.partial(predict_kernel, tiles, nz, per_chunk, chunks, rows, width),
        out_shape=(
            jax.ShapeDtypeStruct((rows + 2 * reach, nt, 2, chunks, 8, LANES), jnp.float32),
            jax.ShapeDtypeStruct((rows, mains, 2, chunks, 8, LANES), jnp.float32),
        ),
        in_specs=[hbm, hbm, hbm, vmem],
        out_specs=(vmem, vmem),
        scratch_shapes=[
            pltpu.VMEM((chunks, 2, 8, full, width), jnp.float32),
            pltpu.VMEM((chunks, nz, full, LANES), jnp.float32),
            pltpu.VMEM((full, width + 2 * LANES), jnp.int32),
            pltpu.VMEM((nt, full, 8, LANES), jnp.int32),
            pltpu.VMEM((4, nt, full, 8, LANES), jnp.float32),
            pltpu.VMEM((2, 2, nt, full, 8, LANES), jnp.float32),
            dma((chunks, nz)), dma((chunks, nz)), dma((chunks, nz)), dma((chunks, nz)),
            dma((chunks, 2)), dma((chunks, 2)), dma((chunks, 2)), dma((chunks, 2)),
            dma((2,)), dma((2,)), dma((chunks + 1, 2)),
        ],
        compiler_params=pltpu.CompilerParams(
            collective_id=0, has_side_effects=True, vmem_limit_bytes=56 * 2**20
        ),
        name="predict",
    )(data_spectrum, strips, levels, table)

    block = pl.BlockSpec((samples, 8, width), lambda i: (0, i, 0))
    out = jax.ShapeDtypeStruct((samples, rows, width), jnp.float32)
    return pl.pallas_call(
        functools.partial(subtract_kernel, rows, width),
        grid=(rows // 8,),
        out_shape=(out, out),
        in_specs=[vmem, vmem, vmem],
        out_specs=(block, block),
        scratch_shapes=[
            pltpu.VMEM((2 * reach + 1, rows + 2 * reach, samples, width), jnp.float32),
            pltpu.VMEM((8, samples, width), jnp.float32),
            pltpu.VMEM((8, samples, width), jnp.float32),
        ],
        compiler_params=pltpu.CompilerParams(vmem_limit_bytes=56 * 2**20),
        name="subtract",
    )(predicted, recorded, basis)


def solution(mesh):
    in_specs = (P(None, "freq", "tile", None), P("tile", None))
    out_specs = (P(None, "tile", "freq"), P(None, "tile", "freq"))
    return jax.shard_map(
        functools.partial(local, dict(mesh.shape)),
        mesh=mesh, in_specs=in_specs, out_specs=out_specs, check_vma=False,
    )
```

```python
import functools
import math

import jax
import jax.numpy as jnp
import ml_dtypes
import numpy as np
from jax import lax
from jax.experimental import pallas as pl
from jax.experimental.pallas import tpu as pltpu
from jax.sharding import PartitionSpec as P

GROUPS = 3
PASSES = 3
STEPS = 4 * GROUPS

damping = 0.2
paraxial_top = 0.1
depth_step = 10.0
cell_width = 12.5
step_size = 0.6
energy_floor = 1e-05
filter_reach = 2

HALO = 16
LANES = 128
ROWS = 8
STRIDE = 100
OUTSIDE = 127
MESH = pl.DeviceIdType.MESH


def tile_count(width):
    count = 1
    while STRIDE * count < width + filter_reach + 1:
        count += 1
    return count


def overlapped(pieces, tile, lane):
    origin = STRIDE * tile - HALO + LANES
    k, off = origin // LANES, origin % LANES
    turn = LANES - off
    axis = pieces[0].ndim - 1
    return jnp.where(
        lane < turn, pltpu.roll(pieces[k], turn, axis), pltpu.roll(pieces[k + 1], turn, axis)
    )


def coefficient_table(orders, nz, per_chunk, chunks):
    table = np.zeros((chunks, 4, 8, LANES), np.float64)
    velocity = 1500.0 + 250.0 * np.arange(OUTSIDE)
    for j in range(chunks):
        for s in range(nz):
            for i in range(per_chunk):
                k = s * (orders // nz) + j * per_chunk + i
                omega = 4.0 * math.pi * (k + 1)
                theta = omega * depth_step / velocity
                q = velocity / (omega * cell_width)
                spread = damping + 1j * paraxial_top * q / (1.0 + q)
                turn = np.exp(1j * theta)
                centre = turn * (1.0 - 4.0 * spread)
                beside = turn * spread
                table[j, :, s * per_chunk + i, :OUTSIDE] = np.stack(
                    [centre.real, centre.imag, beside.real, beside.imag]
                )
    return table.astype(np.float32)


def trace_basis(orders, nz, per_chunk, chunks):
    samples = 2 * orders
    times = np.arange(samples)[:, None] + 0.5
    order = [
        s * (orders // nz) + j * per_chunk + i
        for j in range(chunks)
        for s in range(nz)
        for i in range(per_chunk)
    ]
    angles = 2.0 * math.pi * (np.array(order)[None, :] + 1.0) * times / samples
    basis = np.concatenate([np.cos(angles), -np.sin(angles)], axis=1) / math.sqrt(orders)
    basis = basis.astype(np.float32)
    high = basis.astype(ml_dtypes.bfloat16)
    low = (basis - high.astype(np.float32)).astype(ml_dtypes.bfloat16)
    return np.concatenate([high, high, low, low], axis=1)


def predict_kernel(
    tiles, nz, per_chunk, chunks, rows, width,
    x_ref, strip_ref, level_ref, table_ref,
    m_ref, d_ref,
    ext, sext, lext, index, coef, state, other,
    a_send, a_recv, s_send, s_recv, r_send, r_recv, q_send, q_recv, l_send, l_recv, own,
):
    tile = lax.axis_index("tile")
    me = lax.axis_index("freq")
    has_up = tile > 0
    has_down = tile < tiles - 1
    nt = tile_count(width)
    mains = width // LANES
    full = rows + 2 * HALO
    inner = pl.ds(HALO, rows)
    window = pl.ds(pl.multiple_of(me * width, LANES), width + 2 * LANES)

    barrier = pltpu.get_barrier_semaphore()
    for hop in range(1, nz):
        pl.semaphore_signal(
            barrier, inc=1, device_id=(tile, lax.rem(me + hop, nz)), device_id_type=MESH
        )

    @pl.when(has_up)
    def _():
        pl.semaphore_signal(barrier, inc=1, device_id=(tile - 1, me), device_id_type=MESH)

    @pl.when(has_down)
    def _():
        pl.semaphore_signal(barrier, inc=1, device_id=(tile + 1, me), device_id_type=MESH)

    pl.semaphore_wait(
        barrier, nz - 1 + has_up.astype(jnp.int32) + has_down.astype(jnp.int32)
    )

    def level_copy(up):
        src = level_ref.at[pl.ds(0 if up else rows - HALO, HALO), window]
        dst = lext.at[pl.ds(HALO + rows if up else 0, HALO), :]
        way = 0 if up else 1
        return pltpu.make_async_remote_copy(
            src_ref=src, dst_ref=dst, send_sem=l_send.at[way], recv_sem=l_recv.at[way],
            device_id=(tile + (-1 if up else 1), me), device_id_type=MESH,
        )

    def main_copy(j, dest, source):
        return pltpu.make_async_remote_copy(
            src_ref=x_ref.at[
                :, pl.ds(j * per_chunk, per_chunk), :,
                pl.ds(pl.multiple_of(dest * width, LANES), width),
            ],
            dst_ref=ext.at[j, :, pl.ds(source * per_chunk, per_chunk), inner, :],
            send_sem=a_send.at[j, dest], recv_sem=a_recv.at[j, source],
            device_id=(tile, dest), device_id_type=MESH,
        )

    def strip_copy(j, dest, source):
        return pltpu.make_async_remote_copy(
            src_ref=strip_ref.at[dest, j],
            dst_ref=sext.at[j, source, inner, :],
            send_sem=s_send.at[j, dest], recv_sem=s_recv.at[j, source],
            device_id=(tile, dest), device_id_type=MESH,
        )

    def row_copies(j, up):
        src = pl.ds(HALO if up else rows, HALO)
        dst = pl.ds(HALO + rows if up else 0, HALO)
        way = 0 if up else 1
        target = (tile + (-1 if up else 1), me)
        return (
            pltpu.make_async_remote_copy(
                src_ref=ext.at[j, :, :, src, :], dst_ref=ext.at[j, :, :, dst, :],
                send_sem=r_send.at[j, way], recv_sem=r_recv.at[j, way],
                device_id=target, device_id_type=MESH,
            ),
            pltpu.make_async_remote_copy(
                src_ref=sext.at[j, :, src, :], dst_ref=sext.at[j, :, dst, :],
                send_sem=q_send.at[j, way], recv_sem=q_recv.at[j, way],
                device_id=target, device_id_type=MESH,
            ),
        )

    def own_copies(j):
        return (
            pltpu.make_async_copy(
                x_ref.at[
                    :, pl.ds(j * per_chunk, per_chunk), :,
                    pl.ds(pl.multiple_of(me * width, LANES), width),
                ],
                ext.at[j, :, pl.ds(me * per_chunk, per_chunk), inner, :],
                own.at[j, 0],
            ),
            pltpu.make_async_copy(
                strip_ref.at[me, j], sext.at[j, me, inner, :], own.at[j, 1]
            ),
        )

    own_level = pltpu.make_async_copy(
        level_ref.at[:, window], lext.at[inner, :], own.at[chunks, 0]
    )

    @pl.when(has_up)
    def _():
        level_copy(True).start()

    @pl.when(has_down)
    def _():
        level_copy(False).start()

    own_level.start()

    def send(j, carry):
        for hop in range(1, nz):
            dest = lax.rem(me + hop, nz)
            strip_copy(j, dest, me).start()
            main_copy(j, dest, me).start()
        for copy in own_copies(j):
            copy.start()
        return carry

    lax.fori_loop(0, chunks, send, 0)

    top, bottom = pl.ds(0, HALO), pl.ds(HALO + rows, HALO)
    for missing, edge in ((jnp.logical_not(has_up), top), (jnp.logical_not(has_down), bottom)):

        @pl.when(missing)
        def _(edge=edge):
            lext[edge, :] = jnp.full((HALO, lext.shape[1]), OUTSIDE, jnp.int32)

            def clear(j, carry):
                for part in range(2):
                    for f in range(8):
                        ext[j, part, f, edge, :] = jnp.zeros((HALO, width), jnp.float32)
                for s in range(nz):
                    sext[j, s, edge, :] = jnp.zeros((HALO, LANES), jnp.float32)
                return carry

            lax.fori_loop(0, chunks, clear, 0)

    own_level.wait()

    @pl.when(has_up)
    def _():
        level_copy(True).wait_send()
        level_copy(False).wait_recv()

    @pl.when(has_down)
    def _():
        level_copy(False).wait_send()
        level_copy(True).wait_recv()

    lane2 = lax.broadcasted_iota(jnp.int32, (8, LANES), 1)
    lane3 = lax.broadcasted_iota(jnp.int32, (8, 8, LANES), 2)

    def make_index(b, carry):
        at = pl.ds(pl.multiple_of(b * 8, 8), 8)
        pieces = [lext[at, k * LANES : (k + 1) * LANES] for k in range(mains + 2)]
        for t in range(nt):
            found = overlapped(pieces, t, lane2)
            index[t, at] = jnp.broadcast_to(found[:, None, :], (8, 8, LANES))
        return carry

    lax.fori_loop(0, full // 8, make_index, 0)

    def one_chunk(j, carry):
        for copy in own_copies(j):
            copy.wait()
        for hop in range(1, nz):
            source = lax.rem(me + hop, nz)
            main_copy(j, me, source).wait_recv()
            strip_copy(j, me, source).wait_recv()

        @pl.when(has_up)
        def _():
            for copy in row_copies(j, True):
                copy.start()

        @pl.when(has_down)
        def _():
            for copy in row_copies(j, False):
                copy.start()

        def make_coef(b, carry):
            values = [table_ref[j, c] for c in range(4)]
            for r in range(8):
                for t in range(nt):
                    at = index[t, 8 * b + r]
                    for c in range(4):
                        coef[c, t, 8 * b + r] = jnp.take_along_axis(
                            values[c], at, axis=1, mode="promise_in_bounds"
                        )
            return carry

        lax.fori_loop(0, full // 8, make_coef, 0)

        @pl.when(has_up)
        def _():
            for copy in row_copies(j, False):
                copy.wait_recv()

        @pl.when(has_down)
        def _():
            for copy in row_copies(j, True):
                copy.wait_recv()

        def fill(b, carry):
            at = pl.ds(pl.multiple_of(b * 8, 8), 8)
            for part in range(2):
                main = [
                    jnp.swapaxes(ext[j, part, :, at, k * LANES : (k + 1) * LANES], 0, 1)
                    for k in range(mains)
                ]
                strips = []
                for s in range(nz):
                    strip = sext[j, s, at, :]
                    for i in range(per_chunk):
                        base = (part * per_chunk + i) * 2 * HALO
                        strips.append(pltpu.roll(strip, (LANES - base - HALO) % LANES, 1))
                strip = jnp.swapaxes(jnp.stack(strips), 0, 1)
                pieces = [strip] + main + [strip]
                for t in range(nt):
                    state[part, t, at] = overlapped(pieces, t, lane3)

                @pl.when((b >= HALO // 8) & (b < (HALO + rows) // 8))
                def _():
                    for k in range(mains):
                        for r in range(8):
                            d_ref[b * 8 - HALO + r, k, part, j] = main[k][r]
            return carry

        lax.fori_loop(0, full // 8, fill, 0)

        def one_step(s, old, new):
            first = HALO - filter_reach - STEPS + s
            count = rows + 2 * (filter_reach + STEPS) - 2 * s

            def block(b, carry):
                e = first + ROWS * b
                for t in range(nt):
                    re = [old[0, t, e - 1 + r] for r in range(ROWS + 2)]
                    im = [old[1, t, e - 1 + r] for r in range(ROWS + 2)]
                    for r in range(ROWS):
                        a, b_ = re[r + 1], im[r + 1]
                        nr = (re[r] + re[r + 2]) + (
                            pltpu.roll(a, 1, 1) + pltpu.roll(a, LANES - 1, 1)
                        )
                        ni = (im[r] + im[r + 2]) + (
                            pltpu.roll(b_, 1, 1) + pltpu.roll(b_, LANES - 1, 1)
                        )
                        cr, ci = coef[0, t, e + r], coef[1, t, e + r]
                        br, bi = coef[2, t, e + r], coef[3, t, e + r]
                        new[0, t, e + r] = (cr * a - ci * b_) + (br * nr - bi * ni)
                        new[1, t, e + r] = (cr * b_ + ci * a) + (br * ni + bi * nr)
                return carry

            lax.fori_loop(0, (count + ROWS - 1) // ROWS, block, 0)

        def two_steps(n, carry):
            one_step(2 * n + 1, state, other)
            one_step(2 * n + 2, other, state)
            return carry

        lax.fori_loop(0, STEPS // 2, two_steps, 0)

        def put(b, carry):
            for r in range(4):
                for t in range(nt):
                    for part in range(2):
                        m_ref[4 * b + r, t, part, j] = state[
                            part, t, 4 * b + r + HALO - filter_reach
                        ]
            return carry

        lax.fori_loop(0, rows // 4 + filter_reach // 2, put, 0)
        return carry

    lax.fori_loop(0, chunks, one_chunk, 0)

    def finish(j, carry):
        for hop in range(1, nz):
            dest = lax.rem(me + hop, nz)
            strip_copy(j, dest, me).wait_send()
            main_copy(j, dest, me).wait_send()

        @pl.when(has_up)
        def _():
            for copy in row_copies(j, True):
                copy.wait_send()

        @pl.when(has_down)
        def _():
            for copy in row_copies(j, False):
                copy.wait_send()

        return carry

    lax.fori_loop(0, chunks, finish, 0)


def to_trace(basis, spectrum):
    high = spectrum.astype(jnp.bfloat16)
    low = (spectrum - high.astype(jnp.float32)).astype(jnp.bfloat16)
    both = jnp.concatenate([high, low, high, low], axis=0)
    return jnp.dot(basis, both, preferred_element_type=jnp.float32)


def subtract_kernel(rows, width, m_ref, d_ref, basis_ref, p_ref, q_ref, shifted, data, result):
    i = pl.program_id(0)
    mains = width // LANES
    nt = m_ref.shape[1]
    reach = filter_reach
    diameter = 2 * reach + 1
    samples = basis_ref.shape[0]
    basis = basis_ref[...]
    lane = lax.broadcasted_iota(jnp.int32, (samples, LANES), 1)

    def make_row(r, carry):
        spectrum = jnp.concatenate(
            [m_ref[r, t].reshape(samples, LANES) for t in range(nt)], axis=1
        )
        traces = -to_trace(basis, spectrum)
        for shift in range(diameter):
            for b in range(mains):
                low = LANES * b + shift - reach
                value = None
                for t in range(nt):
                    begin, end = STRIDE * t - reach, STRIDE * (t + 1) - reach
                    if end <= low or begin >= low + LANES:
                        continue
                    tile = traces[:, t * LANES : (t + 1) * LANES]
                    turn = (STRIDE * t - HALO - low) % LANES
                    moved = pltpu.roll(tile, turn, 1) if turn else tile
                    value = moved if value is None else jnp.where(lane < begin - low, value, moved)
                shifted[shift, r, :, b * LANES : (b + 1) * LANES] = value
        return carry

    lax.fori_loop(jnp.where(i == 0, 0, 8 * i + 2 * reach), 8 * i + 8 + 2 * reach, make_row, 0)

    def make_data(r, carry):
        spectrum = jnp.concatenate(
            [d_ref[8 * i + r, b].reshape(samples, LANES) for b in range(mains)], axis=1
        )
        data[r] = to_trace(basis, spectrum)
        return carry

    lax.fori_loop(0, 8, make_data, 0)

    taps = [(a, c) for a in range(diameter) for c in range(diameter)]

    def one_row(n, carry):
        r, b = n // mains, lax.rem(n, mains)
        at = pl.ds(pl.multiple_of(b * LANES, LANES), LANES)

        def tap(a, c):
            return shifted[c, 8 * i + r + a, :, at]

        recorded = data[r, :, at]

        def total(values):
            return jnp.sum(values, axis=0, keepdims=True)

        power = jnp.zeros((8, LANES), jnp.float32)
        for a, c in taps:
            value = tap(a, c)
            power = power + jnp.sum((value * value).reshape(samples // 8, 8, LANES), axis=0)
        gain = step_size / (energy_floor + total(power))
        weights = None
        for repeat in range(PASSES):
            residual = recorded
            if weights is not None:
                for weight, (a, c) in zip(weights, taps):
                    residual = residual - weight * tap(a, c)
            change = [total(residual * tap(a, c)) * gain for a, c in taps]
            weights = (
                change if weights is None else [w + more for w, more in zip(weights, change)]
            )
        residual = recorded
        for weight, (a, c) in zip(weights, taps):
            residual = residual - weight * tap(a, c)
        result[r, :, at] = residual
        return carry

    lax.fori_loop(0, 8 * mains, one_row, 0)

    for k in range(samples // 8):
        part = slice(8 * k, 8 * k + 8)
        p_ref[part] = jnp.swapaxes(result[:, part, :], 0, 1)
        q_ref[part] = jnp.swapaxes(
            shifted[reach, pl.ds(8 * i + reach, 8), part, :], 0, 1
        )


def local(mesh_shape, data_spectrum, velocity_level):
    nz, tiles = mesh_shape["freq"], mesh_shape["tile"]
    _, local_freqs, rows, cols = data_spectrum.shape
    orders = local_freqs * nz
    samples = 2 * orders
    width = cols // nz
    per_chunk = 8 // nz
    chunks = local_freqs // per_chunk
    nt = tile_count(width)
    mains = width // LANES
    full = rows + 2 * HALO
    reach = filter_reach

    around = jnp.pad(data_spectrum, ((0, 0), (0, 0), (0, 0), (HALO, HALO)))
    strips = jnp.stack(
        [
            jnp.concatenate(
                [
                    around[..., d * width : d * width + HALO],
                    around[..., (d + 1) * width + HALO : (d + 1) * width + 2 * HALO],
                ],
                axis=-1,
            )
            for d in range(nz)
        ]
    )
    strips = strips.reshape(nz, 2, chunks, per_chunk, rows, 2 * HALO)
    strips = strips.transpose(0, 2, 4, 1, 3, 5).reshape(nz, chunks, rows, -1)
    strips = jnp.pad(strips, ((0, 0),) * 3 + ((0, LANES - strips.shape[-1]),))
    levels = jnp.pad(velocity_level, ((0, 0), (LANES, LANES)), constant_values=OUTSIDE)
    table = jnp.asarray(coefficient_table(orders, nz, per_chunk, chunks))
    basis = jnp.asarray(trace_basis(orders, nz, per_chunk, chunks))

    dma = pltpu.SemaphoreType.DMA
    vmem = pl.BlockSpec(memory_space=pltpu.VMEM)
    hbm = pl.BlockSpec(memory_space=pl.ANY)
    predicted, recorded = pl.pallas_call(
        functools.partial(predict_kernel, tiles, nz, per_chunk, chunks, rows, width),
        out_shape=(
            jax.ShapeDtypeStruct((rows + 2 * reach, nt, 2, chunks, 8, LANES), jnp.float32),
            jax.ShapeDtypeStruct((rows, mains, 2, chunks, 8, LANES), jnp.float32),
        ),
        in_specs=[hbm, hbm, hbm, vmem],
        out_specs=(vmem, vmem),
        scratch_shapes=[
            pltpu.VMEM((chunks, 2, 8, full, width), jnp.float32),
            pltpu.VMEM((chunks, nz, full, LANES), jnp.float32),
            pltpu.VMEM((full, width + 2 * LANES), jnp.int32),
            pltpu.VMEM((nt, full, 8, LANES), jnp.int32),
            pltpu.VMEM((4, nt, full + ROWS, 8, LANES), jnp.float32),
            pltpu.VMEM((2, nt, full + ROWS, 8, LANES), jnp.float32),
            pltpu.VMEM((2, nt, full + ROWS, 8, LANES), jnp.float32),
            dma((chunks, nz)), dma((chunks, nz)), dma((chunks, nz)), dma((chunks, nz)),
            dma((chunks, 2)), dma((chunks, 2)), dma((chunks, 2)), dma((chunks, 2)),
            dma((2,)), dma((2,)), dma((chunks + 1, 2)),
        ],
        compiler_params=pltpu.CompilerParams(
            collective_id=0, has_side_effects=True, vmem_limit_bytes=56 * 2**20
        ),
        name="predict",
    )(data_spectrum, strips, levels, table)

    block = pl.BlockSpec((samples, 8, width), lambda i: (0, i, 0))
    out = jax.ShapeDtypeStruct((samples, rows, width), jnp.float32)
    return pl.pallas_call(
        functools.partial(subtract_kernel, rows, width),
        grid=(rows // 8,),
        out_shape=(out, out),
        in_specs=[vmem, vmem, vmem],
        out_specs=(block, block),
        scratch_shapes=[
            pltpu.VMEM((2 * reach + 1, rows + 2 * reach, samples, width), jnp.float32),
            pltpu.VMEM((8, samples, width), jnp.float32),
            pltpu.VMEM((8, samples, width), jnp.float32),
        ],
        compiler_params=pltpu.CompilerParams(vmem_limit_bytes=56 * 2**20),
        name="subtract",
    )(predicted, recorded, basis)


def solution(mesh):
    in_specs = (P(None, "freq", "tile", None), P("tile", None))
    out_specs = (P(None, "tile", "freq"), P(None, "tile", "freq"))
    return jax.shard_map(
        functools.partial(local, dict(mesh.shape)),
        mesh=mesh, in_specs=in_specs, out_specs=out_specs, check_vma=False,
    )
```

```python
import functools
import math

import jax
import jax.numpy as jnp
import ml_dtypes
import numpy as np
from jax import lax
from jax.experimental import pallas as pl
from jax.experimental.pallas import tpu as pltpu
from jax.sharding import PartitionSpec as P

GROUPS = 3
PASSES = 3
STEPS = 4 * GROUPS

damping = 0.2
paraxial_top = 0.1
depth_step = 10.0
cell_width = 12.5
step_size = 0.6
energy_floor = 1e-05
filter_reach = 2

HALO = 16
LANES = 128
ROWS = 8
STRIDE = 100
OUTSIDE = 127
MESH = pl.DeviceIdType.MESH


def tile_count(width):
    count = 1
    while STRIDE * count < width + filter_reach + 1:
        count += 1
    return count


def overlapped(pieces, tile, lane):
    origin = STRIDE * tile - HALO + LANES
    k, off = origin // LANES, origin % LANES
    turn = LANES - off
    axis = pieces[0].ndim - 1
    return jnp.where(
        lane < turn, pltpu.roll(pieces[k], turn, axis), pltpu.roll(pieces[k + 1], turn, axis)
    )


def coefficient_table(orders, nz, per_chunk, chunks):
    table = np.zeros((chunks, 4, 8, LANES), np.float64)
    velocity = 1500.0 + 250.0 * np.arange(OUTSIDE)
    for j in range(chunks):
        for s in range(nz):
            for i in range(per_chunk):
                k = s * (orders // nz) + j * per_chunk + i
                omega = 4.0 * math.pi * (k + 1)
                theta = omega * depth_step / velocity
                q = velocity / (omega * cell_width)
                spread = damping + 1j * paraxial_top * q / (1.0 + q)
                turn = np.exp(1j * theta)
                centre = turn * (1.0 - 4.0 * spread)
                beside = turn * spread
                table[j, :, s * per_chunk + i, :OUTSIDE] = np.stack(
                    [centre.real, centre.imag, beside.real, beside.imag]
                )
    return table.astype(np.float32)


def trace_basis(orders, nz, per_chunk, chunks):
    samples = 2 * orders
    times = np.arange(samples)[:, None] + 0.5
    order = [
        s * (orders // nz) + j * per_chunk + i
        for j in range(chunks)
        for s in range(nz)
        for i in range(per_chunk)
    ]
    angles = 2.0 * math.pi * (np.array(order)[None, :] + 1.0) * times / samples
    basis = np.concatenate([np.cos(angles), -np.sin(angles)], axis=1) / math.sqrt(orders)
    basis = basis.astype(np.float32)
    high = basis.astype(ml_dtypes.bfloat16)
    low = (basis - high.astype(np.float32)).astype(ml_dtypes.bfloat16)
    return np.concatenate([high, high, low, low], axis=1)


def predict_kernel(
    tiles, nz, per_chunk, chunks, rows, width,
    x_ref, strip_ref, level_ref, table_ref,
    m_ref, d_ref,
    ext, sext, lext, index, coef, state, other,
    a_send, a_recv, s_send, s_recv, r_send, r_recv, q_send, q_recv, l_send, l_recv, own,
):
    tile = lax.axis_index("tile")
    me = lax.axis_index("freq")
    has_up = tile > 0
    has_down = tile < tiles - 1
    nt = tile_count(width)
    mains = width // LANES
    full = rows + 2 * HALO
    inner = pl.ds(HALO, rows)
    window = pl.ds(pl.multiple_of(me * width, LANES), width + 2 * LANES)

    barrier = pltpu.get_barrier_semaphore()
    for hop in range(1, nz):
        pl.semaphore_signal(
            barrier, inc=1, device_id=(tile, lax.rem(me + hop, nz)), device_id_type=MESH
        )

    @pl.when(has_up)
    def _():
        pl.semaphore_signal(barrier, inc=1, device_id=(tile - 1, me), device_id_type=MESH)

    @pl.when(has_down)
    def _():
        pl.semaphore_signal(barrier, inc=1, device_id=(tile + 1, me), device_id_type=MESH)

    pl.semaphore_wait(
        barrier, nz - 1 + has_up.astype(jnp.int32) + has_down.astype(jnp.int32)
    )

    def level_copy(up):
        src = level_ref.at[pl.ds(0 if up else rows - HALO, HALO), window]
        dst = lext.at[pl.ds(HALO + rows if up else 0, HALO), :]
        way = 0 if up else 1
        return pltpu.make_async_remote_copy(
            src_ref=src, dst_ref=dst, send_sem=l_send.at[way], recv_sem=l_recv.at[way],
            device_id=(tile + (-1 if up else 1), me), device_id_type=MESH,
        )

    def main_copy(j, dest, source):
        return pltpu.make_async_remote_copy(
            src_ref=x_ref.at[
                :, pl.ds(j * per_chunk, per_chunk), :,
                pl.ds(pl.multiple_of(dest * width, LANES), width),
            ],
            dst_ref=ext.at[j, :, pl.ds(source * per_chunk, per_chunk), inner, :],
            send_sem=a_send.at[j, dest], recv_sem=a_recv.at[j, source],
            device_id=(tile, dest), device_id_type=MESH,
        )

    def strip_copy(j, dest, source):
        return pltpu.make_async_remote_copy(
            src_ref=strip_ref.at[dest, j],
            dst_ref=sext.at[j, source, inner, :],
            send_sem=s_send.at[j, dest], recv_sem=s_recv.at[j, source],
            device_id=(tile, dest), device_id_type=MESH,
        )

    def row_copies(j, up):
        src = pl.ds(HALO if up else rows, HALO)
        dst = pl.ds(HALO + rows if up else 0, HALO)
        way = 0 if up else 1
        target = (tile + (-1 if up else 1), me)
        return (
            pltpu.make_async_remote_copy(
                src_ref=ext.at[j, :, :, src, :], dst_ref=ext.at[j, :, :, dst, :],
                send_sem=r_send.at[j, way], recv_sem=r_recv.at[j, way],
                device_id=target, device_id_type=MESH,
            ),
            pltpu.make_async_remote_copy(
                src_ref=sext.at[j, :, src, :], dst_ref=sext.at[j, :, dst, :],
                send_sem=q_send.at[j, way], recv_sem=q_recv.at[j, way],
                device_id=target, device_id_type=MESH,
            ),
        )

    def own_copies(j):
        return (
            pltpu.make_async_copy(
                x_ref.at[
                    :, pl.ds(j * per_chunk, per_chunk), :,
                    pl.ds(pl.multiple_of(me * width, LANES), width),
                ],
                ext.at[j, :, pl.ds(me * per_chunk, per_chunk), inner, :],
                own.at[j, 0],
            ),
            pltpu.make_async_copy(
                strip_ref.at[me, j], sext.at[j, me, inner, :], own.at[j, 1]
            ),
        )

    own_level = pltpu.make_async_copy(
        level_ref.at[:, window], lext.at[inner, :], own.at[chunks, 0]
    )

    @pl.when(has_up)
    def _():
        level_copy(True).start()

    @pl.when(has_down)
    def _():
        level_copy(False).start()

    own_level.start()

    def send(j):
        for hop in range(1, nz):
            dest = lax.rem(me + hop, nz)
            strip_copy(j, dest, me).start()
            main_copy(j, dest, me).start()

    def sent(j):
        for hop in range(1, nz):
            dest = lax.rem(me + hop, nz)
            strip_copy(j, dest, me).wait_send()
            main_copy(j, dest, me).wait_send()

    send(0)

    def keep(j, carry):
        for copy in own_copies(j):
            copy.start()
        return carry

    lax.fori_loop(0, chunks, keep, 0)

    top, bottom = pl.ds(0, HALO), pl.ds(HALO + rows, HALO)
    for missing, edge in ((jnp.logical_not(has_up), top), (jnp.logical_not(has_down), bottom)):

        @pl.when(missing)
        def _(edge=edge):
            lext[edge, :] = jnp.full((HALO, lext.shape[1]), OUTSIDE, jnp.int32)

            def clear(j, carry):
                for part in range(2):
                    for f in range(8):
                        ext[j, part, f, edge, :] = jnp.zeros((HALO, width), jnp.float32)
                for s in range(nz):
                    sext[j, s, edge, :] = jnp.zeros((HALO, LANES), jnp.float32)
                return carry

            lax.fori_loop(0, chunks, clear, 0)

    own_level.wait()

    @pl.when(has_up)
    def _():
        level_copy(True).wait_send()
        level_copy(False).wait_recv()

    @pl.when(has_down)
    def _():
        level_copy(False).wait_send()
        level_copy(True).wait_recv()

    lane2 = lax.broadcasted_iota(jnp.int32, (8, LANES), 1)
    lane3 = lax.broadcasted_iota(jnp.int32, (8, 8, LANES), 2)

    def make_index(b, carry):
        at = pl.ds(pl.multiple_of(b * 8, 8), 8)
        pieces = [lext[at, k * LANES : (k + 1) * LANES] for k in range(mains + 2)]
        for t in range(nt):
            found = overlapped(pieces, t, lane2)
            index[t, at] = jnp.broadcast_to(found[:, None, :], (8, 8, LANES))
        return carry

    lax.fori_loop(0, full // 8, make_index, 0)

    def one_chunk(j, carry):
        sent(j)

        @pl.when(j + 1 < chunks)
        def _():
            send(j + 1)

        for copy in own_copies(j):
            copy.wait()
        for hop in range(1, nz):
            source = lax.rem(me + hop, nz)
            main_copy(j, me, source).wait_recv()
            strip_copy(j, me, source).wait_recv()

        @pl.when(has_up)
        def _():
            for copy in row_copies(j, True):
                copy.start()

        @pl.when(has_down)
        def _():
            for copy in row_copies(j, False):
                copy.start()

        def make_coef(b, carry):
            values = [table_ref[j, c] for c in range(4)]
            for r in range(8):
                for t in range(nt):
                    at = index[t, 8 * b + r]
                    for c in range(4):
                        coef[c, t, 8 * b + r] = jnp.take_along_axis(
                            values[c], at, axis=1, mode="promise_in_bounds"
                        )
            return carry

        lax.fori_loop(0, full // 8, make_coef, 0)

        @pl.when(has_up)
        def _():
            for copy in row_copies(j, False):
                copy.wait_recv()

        @pl.when(has_down)
        def _():
            for copy in row_copies(j, True):
                copy.wait_recv()

        def fill(b, carry):
            at = pl.ds(pl.multiple_of(b * 8, 8), 8)
            for part in range(2):
                main = [
                    jnp.swapaxes(ext[j, part, :, at, k * LANES : (k + 1) * LANES], 0, 1)
                    for k in range(mains)
                ]
                strips = []
                for s in range(nz):
                    strip = sext[j, s, at, :]
                    for i in range(per_chunk):
                        base = (part * per_chunk + i) * 2 * HALO
                        strips.append(pltpu.roll(strip, (LANES - base - HALO) % LANES, 1))
                strip = jnp.swapaxes(jnp.stack(strips), 0, 1)
                pieces = [strip] + main + [strip]
                for t in range(nt):
                    state[part, t, at] = overlapped(pieces, t, lane3)

                @pl.when((b >= HALO // 8) & (b < (HALO + rows) // 8))
                def _():
                    for k in range(mains):
                        for r in range(8):
                            d_ref[b * 8 - HALO + r, k, part, j] = main[k][r]
            return carry

        lax.fori_loop(0, full // 8, fill, 0)

        def one_step(s, old, new):
            first = HALO - filter_reach - STEPS + s
            count = rows + 2 * (filter_reach + STEPS) - 2 * s

            def block(b, carry):
                e = first + ROWS * b
                for t in range(nt):
                    re = [old[0, t, e - 1 + r] for r in range(ROWS + 2)]
                    im = [old[1, t, e - 1 + r] for r in range(ROWS + 2)]
                    for r in range(ROWS):
                        a, b_ = re[r + 1], im[r + 1]
                        nr = (re[r] + re[r + 2]) + (
                            pltpu.roll(a, 1, 1) + pltpu.roll(a, LANES - 1, 1)
                        )
                        ni = (im[r] + im[r + 2]) + (
                            pltpu.roll(b_, 1, 1) + pltpu.roll(b_, LANES - 1, 1)
                        )
                        cr, ci = coef[0, t, e + r], coef[1, t, e + r]
                        br, bi = coef[2, t, e + r], coef[3, t, e + r]
                        new[0, t, e + r] = (cr * a - ci * b_) + (br * nr - bi * ni)
                        new[1, t, e + r] = (cr * b_ + ci * a) + (br * ni + bi * nr)
                return carry

            lax.fori_loop(0, (count + ROWS - 1) // ROWS, block, 0)

        def two_steps(n, carry):
            one_step(2 * n + 1, state, other)
            one_step(2 * n + 2, other, state)
            return carry

        lax.fori_loop(0, STEPS // 2, two_steps, 0)

        def put(b, carry):
            for r in range(4):
                for t in range(nt):
                    for part in range(2):
                        m_ref[4 * b + r, t, part, j] = state[
                            part, t, 4 * b + r + HALO - filter_reach
                        ]
            return carry

        lax.fori_loop(0, (rows + 8) // 4, put, 0)
        return carry

    lax.fori_loop(0, chunks, one_chunk, 0)

    def finish(j, carry):
        @pl.when(has_up)
        def _():
            for copy in row_copies(j, True):
                copy.wait_send()

        @pl.when(has_down)
        def _():
            for copy in row_copies(j, False):
                copy.wait_send()

        return carry

    lax.fori_loop(0, chunks, finish, 0)


def to_trace(basis, spectrum):
    high = spectrum.astype(jnp.bfloat16)
    low = (spectrum - high.astype(jnp.float32)).astype(jnp.bfloat16)
    both = jnp.concatenate([high, low, high, low], axis=0)
    return jnp.dot(basis, both, preferred_element_type=jnp.float32)


def subtract_kernel(
    rows, width, m_ref, d_ref, basis_ref, p_ref, q_ref, shifted, power, data, residual, held
):
    i = pl.program_id(0)
    mains = width // LANES
    nt = m_ref.shape[1]
    reach = filter_reach
    diameter = 2 * reach + 1
    samples = basis_ref.shape[0]
    basis = basis_ref[...]
    lane = lax.broadcasted_iota(jnp.int32, (8, 8, LANES), 2)

    def traces(ref, first, count):
        def two_rows(n, carry):
            spectrum = jnp.concatenate(
                [
                    ref[first + 2 * n + r, t].reshape(samples, LANES)
                    for r in range(2)
                    for t in range(count)
                ],
                axis=1,
            )
            found = to_trace(basis, spectrum)
            for r in range(2):
                for t in range(count):
                    k = r * count + t
                    held[t, 2 * n + r] = found[:, k * LANES : (k + 1) * LANES]
            return carry

        lax.fori_loop(0, 4, two_rows, 0)

    def make_block(k, carry):
        traces(m_ref, 8 * k, nt)
        here = pl.ds(pl.multiple_of(8 * k, 8), 8)

        def some_times(n, sums):
            at = pl.ds(pl.multiple_of(8 * n, 8), 8)
            tiles = [-jnp.swapaxes(held[t, :, at, :], 0, 1) for t in range(nt)]
            sums = list(sums)
            for shift in range(diameter):
                for b in range(mains):
                    low = LANES * b + shift - reach
                    value = None
                    for t in range(nt):
                        begin, end = STRIDE * t - reach, STRIDE * (t + 1) - reach
                        if end <= low or begin >= low + LANES:
                            continue
                        turn = (STRIDE * t - HALO - low) % LANES
                        moved = pltpu.roll(tiles[t], turn, 2) if turn else tiles[t]
                        value = (
                            moved
                            if value is None
                            else jnp.where(lane < begin - low, value, moved)
                        )
                    shifted[shift, at, b, here, :] = value
                    sums[b] = sums[b] + jnp.sum(value * value, axis=0)
            return tuple(sums)

        zero = jnp.zeros((8, LANES), jnp.float32)
        sums = lax.fori_loop(0, samples // 8, some_times, (zero,) * mains)
        for b in range(mains):
            power[b, here, :] = sums[b]
        return carry

    lax.fori_loop(jnp.where(i == 0, 0, i + 1), i + 2, make_block, 0)

    traces(d_ref, 8 * i, mains)

    def turn_data(n, carry):
        at = pl.ds(pl.multiple_of(8 * n, 8), 8)
        for b in range(mains):
            data[at, b] = jnp.swapaxes(held[b, :, at, :], 0, 1)
        return carry

    lax.fori_loop(0, samples // 8, turn_data, 0)

    taps = [(a, c) for a in range(diameter) for c in range(diameter)]

    def one_tile(b, carry):
        def tap(t, a, c):
            return shifted[c, t, b, pl.ds(8 * i + a, 8), :]

        energy = energy_floor
        for a in range(diameter):
            energy = energy + power[b, pl.ds(8 * i + a, 8), :]
        gain = step_size / energy

        def match(read):
            def some(n, sums):
                sums = list(sums)
                for u in range(2):
                    t = 2 * n + u
                    value = read(t)
                    sums = [sums[k] + value * tap(t, a, c) for k, (a, c) in enumerate(taps)]
                return tuple(sums)

            zero = jnp.zeros((8, LANES), jnp.float32)
            sums = lax.fori_loop(0, samples // 2, some, (zero,) * len(taps))
            return [found * gain for found in sums]

        def remove(weights, write):
            def some(n, carry):
                for u in range(2):
                    t = 2 * n + u
                    parts = [None] * diameter
                    for weight, (a, c) in zip(weights, taps):
                        term = weight * tap(t, a, c)
                        parts[c] = term if parts[c] is None else parts[c] + term
                    filtered = functools.reduce(jnp.add, parts)
                    write(t, data[t, b] - filtered)
                return carry

            lax.fori_loop(0, samples // 2, some, 0)

        def keep(t, value):
            residual[t] = value

        at = pl.ds(pl.multiple_of(b * LANES, LANES), LANES)

        def put(t, value):
            p_ref[t, :, at] = value
            q_ref[t, :, at] = tap(t, reach, reach)

        weights = match(lambda t: data[t, b])
        for repeat in range(1, PASSES):
            remove(weights, keep)
            weights = [w + more for w, more in zip(weights, match(lambda t: residual[t]))]
        remove(weights, put)
        return carry

    lax.fori_loop(0, mains, one_tile, 0)


def local(mesh_shape, data_spectrum, velocity_level):
    nz, tiles = mesh_shape["freq"], mesh_shape["tile"]
    _, local_freqs, rows, cols = data_spectrum.shape
    orders = local_freqs * nz
    samples = 2 * orders
    width = cols // nz
    per_chunk = 8 // nz
    chunks = local_freqs // per_chunk
    nt = tile_count(width)
    mains = width // LANES
    full = rows + 2 * HALO
    reach = filter_reach

    around = jnp.pad(data_spectrum, ((0, 0), (0, 0), (0, 0), (HALO, HALO)))
    strips = jnp.stack(
        [
            jnp.concatenate(
                [
                    around[..., d * width : d * width + HALO],
                    around[..., (d + 1) * width + HALO : (d + 1) * width + 2 * HALO],
                ],
                axis=-1,
            )
            for d in range(nz)
        ]
    )
    strips = strips.reshape(nz, 2, chunks, per_chunk, rows, 2 * HALO)
    strips = strips.transpose(0, 2, 4, 1, 3, 5).reshape(nz, chunks, rows, -1)
    strips = jnp.pad(strips, ((0, 0),) * 3 + ((0, LANES - strips.shape[-1]),))
    levels = jnp.pad(velocity_level, ((0, 0), (LANES, LANES)), constant_values=OUTSIDE)
    table = jnp.asarray(coefficient_table(orders, nz, per_chunk, chunks))
    basis = jnp.asarray(trace_basis(orders, nz, per_chunk, chunks))

    dma = pltpu.SemaphoreType.DMA
    vmem = pl.BlockSpec(memory_space=pltpu.VMEM)
    hbm = pl.BlockSpec(memory_space=pl.ANY)
    predicted, recorded = pl.pallas_call(
        functools.partial(predict_kernel, tiles, nz, per_chunk, chunks, rows, width),
        out_shape=(
            jax.ShapeDtypeStruct((rows + 8, nt, 2, chunks, 8, LANES), jnp.float32),
            jax.ShapeDtypeStruct((rows, mains, 2, chunks, 8, LANES), jnp.float32),
        ),
        in_specs=[hbm, hbm, hbm, vmem],
        out_specs=(vmem, vmem),
        scratch_shapes=[
            pltpu.VMEM((chunks, 2, 8, full, width), jnp.float32),
            pltpu.VMEM((chunks, nz, full, LANES), jnp.float32),
            pltpu.VMEM((full, width + 2 * LANES), jnp.int32),
            pltpu.VMEM((nt, full, 8, LANES), jnp.int32),
            pltpu.VMEM((4, nt, full + ROWS, 8, LANES), jnp.float32),
            pltpu.VMEM((2, nt, full + ROWS, 8, LANES), jnp.float32),
            pltpu.VMEM((2, nt, full + ROWS, 8, LANES), jnp.float32),
            dma((chunks, nz)), dma((chunks, nz)), dma((chunks, nz)), dma((chunks, nz)),
            dma((chunks, 2)), dma((chunks, 2)), dma((chunks, 2)), dma((chunks, 2)),
            dma((2,)), dma((2,)), dma((chunks + 1, 2)),
        ],
        compiler_params=pltpu.CompilerParams(
            collective_id=0, has_side_effects=True, vmem_limit_bytes=56 * 2**20
        ),
        name="predict",
    )(data_spectrum, strips, levels, table)

    block = pl.BlockSpec((samples, 8, width), lambda i: (0, i, 0))
    out = jax.ShapeDtypeStruct((samples, rows, width), jnp.float32)
    return pl.pallas_call(
        functools.partial(subtract_kernel, rows, width),
        grid=(rows // 8,),
        out_shape=(out, out),
        in_specs=[vmem, vmem, vmem],
        out_specs=(block, block),
        scratch_shapes=[
            pltpu.VMEM((2 * reach + 1, samples, mains, rows + 8, LANES), jnp.float32),
            pltpu.VMEM((mains, rows + 8, LANES), jnp.float32),
            pltpu.VMEM((samples, mains, 8, LANES), jnp.float32),
            pltpu.VMEM((samples, 8, LANES), jnp.float32),
            pltpu.VMEM((nt, 8, samples, LANES), jnp.float32),
        ],
        compiler_params=pltpu.CompilerParams(vmem_limit_bytes=56 * 2**20),
        name="subtract",
    )(predicted, recorded, basis)


def solution(mesh):
    in_specs = (P(None, "freq", "tile", None), P("tile", None))
    out_specs = (P(None, "tile", "freq"), P(None, "tile", "freq"))
    return jax.shard_map(
        functools.partial(local, dict(mesh.shape)),
        mesh=mesh, in_specs=in_specs, out_specs=out_specs, check_vma=False,
    )
```

```python
import functools
import math

import jax
import jax.numpy as jnp
import ml_dtypes
import numpy as np
from jax import lax
from jax.experimental import pallas as pl
from jax.experimental.pallas import tpu as pltpu
from jax.sharding import PartitionSpec as P

GROUPS = 3
PASSES = 3
STEPS = 4 * GROUPS

damping = 0.2
paraxial_top = 0.1
depth_step = 10.0
cell_width = 12.5
step_size = 0.6
energy_floor = 1e-05
filter_reach = 2

HALO = 16
LANES = 128
ROWS = 12
STRIDE = 100
OUTSIDE = 127
MESH = pl.DeviceIdType.MESH


def tile_count(width):
    count = 1
    while STRIDE * count < width + filter_reach + 1:
        count += 1
    return count


def overlapped(pieces, tile, lane):
    origin = STRIDE * tile - HALO + LANES
    k, off = origin // LANES, origin % LANES
    turn = LANES - off
    axis = pieces[0].ndim - 1
    return jnp.where(
        lane < turn, pltpu.roll(pieces[k], turn, axis), pltpu.roll(pieces[k + 1], turn, axis)
    )


def coefficient_table(orders, nz, per_chunk, chunks):
    table = np.zeros((chunks, 4, 8, LANES), np.float64)
    velocity = 1500.0 + 250.0 * np.arange(OUTSIDE)
    for j in range(chunks):
        for s in range(nz):
            for i in range(per_chunk):
                k = s * (orders // nz) + j * per_chunk + i
                omega = 4.0 * math.pi * (k + 1)
                theta = omega * depth_step / velocity
                q = velocity / (omega * cell_width)
                spread = damping + 1j * paraxial_top * q / (1.0 + q)
                turn = np.exp(1j * theta)
                centre = turn * (1.0 - 4.0 * spread)
                beside = turn * spread
                table[j, :, s * per_chunk + i, :OUTSIDE] = np.stack(
                    [centre.real, centre.imag, beside.real, beside.imag]
                )
    return table.astype(np.float32)


def trace_basis(orders, nz, per_chunk, chunks):
    samples = 2 * orders
    times = np.arange(samples)[:, None] + 0.5
    order = [
        s * (orders // nz) + j * per_chunk + i
        for j in range(chunks)
        for s in range(nz)
        for i in range(per_chunk)
    ]
    angles = 2.0 * math.pi * (np.array(order)[None, :] + 1.0) * times / samples
    basis = np.concatenate([np.cos(angles), -np.sin(angles)], axis=1) / math.sqrt(orders)
    basis = basis.astype(np.float32)
    high = basis.astype(ml_dtypes.bfloat16)
    low = (basis - high.astype(np.float32)).astype(ml_dtypes.bfloat16)
    return np.concatenate([high, high, low, low], axis=1)


def predict_kernel(
    tiles, nz, per_chunk, chunks, rows, width,
    x_ref, strip_ref, level_ref, table_ref,
    m_ref, d_ref,
    ext, sext, lext, index, coef, state, other,
    a_send, a_recv, s_send, s_recv, r_send, r_recv, q_send, q_recv, l_send, l_recv, own,
):
    tile = lax.axis_index("tile")
    me = lax.axis_index("freq")
    has_up = tile > 0
    has_down = tile < tiles - 1
    nt = tile_count(width)
    mains = width // LANES
    full = rows + 2 * HALO
    inner = pl.ds(HALO, rows)
    window = pl.ds(pl.multiple_of(me * width, LANES), width + 2 * LANES)

    barrier = pltpu.get_barrier_semaphore()
    for hop in range(1, nz):
        pl.semaphore_signal(
            barrier, inc=1, device_id=(tile, lax.rem(me + hop, nz)), device_id_type=MESH
        )

    @pl.when(has_up)
    def _():
        pl.semaphore_signal(barrier, inc=1, device_id=(tile - 1, me), device_id_type=MESH)

    @pl.when(has_down)
    def _():
        pl.semaphore_signal(barrier, inc=1, device_id=(tile + 1, me), device_id_type=MESH)

    pl.semaphore_wait(
        barrier, nz - 1 + has_up.astype(jnp.int32) + has_down.astype(jnp.int32)
    )

    def level_copy(up):
        src = level_ref.at[pl.ds(0 if up else rows - HALO, HALO), window]
        dst = lext.at[pl.ds(HALO + rows if up else 0, HALO), :]
        way = 0 if up else 1
        return pltpu.make_async_remote_copy(
            src_ref=src, dst_ref=dst, send_sem=l_send.at[way], recv_sem=l_recv.at[way],
            device_id=(tile + (-1 if up else 1), me), device_id_type=MESH,
        )

    def main_copy(j, dest, source):
        return pltpu.make_async_remote_copy(
            src_ref=x_ref.at[
                :, pl.ds(j * per_chunk, per_chunk), :,
                pl.ds(pl.multiple_of(dest * width, LANES), width),
            ],
            dst_ref=ext.at[j, :, pl.ds(source * per_chunk, per_chunk), inner, :],
            send_sem=a_send.at[j, dest], recv_sem=a_recv.at[j, source],
            device_id=(tile, dest), device_id_type=MESH,
        )

    def strip_copy(j, dest, source):
        return pltpu.make_async_remote_copy(
            src_ref=strip_ref.at[dest, j],
            dst_ref=sext.at[j, source, inner, :],
            send_sem=s_send.at[j, dest], recv_sem=s_recv.at[j, source],
            device_id=(tile, dest), device_id_type=MESH,
        )

    def row_copies(j, up):
        src = pl.ds(HALO if up else rows, HALO)
        dst = pl.ds(HALO + rows if up else 0, HALO)
        way = 0 if up else 1
        target = (tile + (-1 if up else 1), me)
        return (
            pltpu.make_async_remote_copy(
                src_ref=ext.at[j, :, :, src, :], dst_ref=ext.at[j, :, :, dst, :],
                send_sem=r_send.at[j, way], recv_sem=r_recv.at[j, way],
                device_id=target, device_id_type=MESH,
            ),
            pltpu.make_async_remote_copy(
                src_ref=sext.at[j, :, src, :], dst_ref=sext.at[j, :, dst, :],
                send_sem=q_send.at[j, way], recv_sem=q_recv.at[j, way],
                device_id=target, device_id_type=MESH,
            ),
        )

    def own_copies(j):
        return (
            pltpu.make_async_copy(
                x_ref.at[
                    :, pl.ds(j * per_chunk, per_chunk), :,
                    pl.ds(pl.multiple_of(me * width, LANES), width),
                ],
                ext.at[j, :, pl.ds(me * per_chunk, per_chunk), inner, :],
                own.at[j, 0],
            ),
            pltpu.make_async_copy(
                strip_ref.at[me, j], sext.at[j, me, inner, :], own.at[j, 1]
            ),
        )

    own_level = pltpu.make_async_copy(
        level_ref.at[:, window], lext.at[inner, :], own.at[chunks, 0]
    )

    @pl.when(has_up)
    def _():
        level_copy(True).start()

    @pl.when(has_down)
    def _():
        level_copy(False).start()

    own_level.start()

    def send(j):
        for hop in range(1, nz):
            dest = lax.rem(me + hop, nz)
            strip_copy(j, dest, me).start()
            main_copy(j, dest, me).start()

    def sent(j):
        for hop in range(1, nz):
            dest = lax.rem(me + hop, nz)
            strip_copy(j, dest, me).wait_send()
            main_copy(j, dest, me).wait_send()

    send(0)

    def keep(j, carry):
        for copy in own_copies(j):
            copy.start()
        return carry

    lax.fori_loop(0, chunks, keep, 0)

    top, bottom = pl.ds(0, HALO), pl.ds(HALO + rows, HALO)
    for missing, edge in ((jnp.logical_not(has_up), top), (jnp.logical_not(has_down), bottom)):

        @pl.when(missing)
        def _(edge=edge):
            lext[edge, :] = jnp.full((HALO, lext.shape[1]), OUTSIDE, jnp.int32)

            def clear(j, carry):
                for part in range(2):
                    for f in range(8):
                        ext[j, part, f, edge, :] = jnp.zeros((HALO, width), jnp.float32)
                for s in range(nz):
                    sext[j, s, edge, :] = jnp.zeros((HALO, LANES), jnp.float32)
                return carry

            lax.fori_loop(0, chunks, clear, 0)

    own_level.wait()

    @pl.when(has_up)
    def _():
        level_copy(True).wait_send()
        level_copy(False).wait_recv()

    @pl.when(has_down)
    def _():
        level_copy(False).wait_send()
        level_copy(True).wait_recv()

    lane2 = lax.broadcasted_iota(jnp.int32, (8, LANES), 1)
    lane3 = lax.broadcasted_iota(jnp.int32, (8, 8, LANES), 2)

    def make_index(b, carry):
        at = pl.ds(pl.multiple_of(b * 8, 8), 8)
        pieces = [lext[at, k * LANES : (k + 1) * LANES] for k in range(mains + 2)]
        for t in range(nt):
            found = overlapped(pieces, t, lane2)
            index[t, at] = jnp.broadcast_to(found[:, None, :], (8, 8, LANES))
        return carry

    lax.fori_loop(0, full // 8, make_index, 0)

    def arrive(j):
        sent(j)

        @pl.when(j + 1 < chunks)
        def _():
            send(j + 1)

        for copy in own_copies(j):
            copy.wait()
        for hop in range(1, nz):
            source = lax.rem(me + hop, nz)
            main_copy(j, me, source).wait_recv()
            strip_copy(j, me, source).wait_recv()

        @pl.when(has_up)
        def _():
            for copy in row_copies(j, True):
                copy.start()

        @pl.when(has_down)
        def _():
            for copy in row_copies(j, False):
                copy.start()

    arrive(0)

    def one_chunk(j, carry):
        def make_coef(b, carry):
            values = [table_ref[j, c] for c in range(4)]
            for r in range(8):
                for t in range(nt):
                    at = index[t, 8 * b + r]
                    for c in range(4):
                        coef[c, t, 8 * b + r] = jnp.take_along_axis(
                            values[c], at, axis=1, mode="promise_in_bounds"
                        )
            return carry

        lax.fori_loop(0, full // 8, make_coef, 0)

        @pl.when(has_up)
        def _():
            for copy in row_copies(j, False):
                copy.wait_recv()

        @pl.when(has_down)
        def _():
            for copy in row_copies(j, True):
                copy.wait_recv()

        def fill(b, carry):
            at = pl.ds(pl.multiple_of(b * 8, 8), 8)
            for part in range(2):
                main = [
                    jnp.swapaxes(ext[j, part, :, at, k * LANES : (k + 1) * LANES], 0, 1)
                    for k in range(mains)
                ]
                strips = []
                for s in range(nz):
                    strip = sext[j, s, at, :]
                    for i in range(per_chunk):
                        base = (part * per_chunk + i) * 2 * HALO
                        strips.append(pltpu.roll(strip, (LANES - base - HALO) % LANES, 1))
                strip = jnp.swapaxes(jnp.stack(strips), 0, 1)
                pieces = [strip] + main + [strip]
                for t in range(nt):
                    state[part, t, at] = overlapped(pieces, t, lane3)

                @pl.when((b >= HALO // 8) & (b < (HALO + rows) // 8))
                def _():
                    for k in range(mains):
                        for r in range(8):
                            d_ref[b * 8 - HALO + r, k, part, j] = main[k][r]
            return carry

        lax.fori_loop(0, full // 8, fill, 0)

        def one_step(s, old, new):
            first = HALO - filter_reach - STEPS + s
            count = rows + 2 * (filter_reach + STEPS) - 2 * s

            def block(b, carry):
                e = first + ROWS * b

                def row(r):
                    return [(old[0, t, e + r], old[1, t, e + r]) for t in range(nt)]

                above, here = row(-1), row(0)
                for r in range(ROWS):
                    below = row(r + 1)
                    for t in range(nt):
                        p, q = here[t]
                        nr = (above[t][0] + below[t][0]) + (
                            pltpu.roll(p, 1, 1) + pltpu.roll(p, LANES - 1, 1)
                        )
                        ni = (above[t][1] + below[t][1]) + (
                            pltpu.roll(q, 1, 1) + pltpu.roll(q, LANES - 1, 1)
                        )
                        cr, ci = coef[0, t, e + r], coef[1, t, e + r]
                        br, bi = coef[2, t, e + r], coef[3, t, e + r]
                        new[0, t, e + r] = (cr * p - ci * q) + (br * nr - bi * ni)
                        new[1, t, e + r] = (cr * q + ci * p) + (br * ni + bi * nr)
                    above, here = here, below
                return carry

            lax.fori_loop(0, (count + ROWS - 1) // ROWS, block, 0)

        def two_steps(n, carry):
            @pl.when((n == STEPS // 2 - 1) & (j + 1 < chunks))
            def _():
                arrive(j + 1)

            one_step(2 * n + 1, state, other)
            one_step(2 * n + 2, other, state)
            return carry

        lax.fori_loop(0, STEPS // 2, two_steps, 0)

        def put(b, carry):
            for r in range(4):
                for t in range(nt):
                    for part in range(2):
                        m_ref[4 * b + r, t, part, j] = state[
                            part, t, 4 * b + r + HALO - filter_reach
                        ]
            return carry

        lax.fori_loop(0, (rows + 8) // 4, put, 0)
        return carry

    lax.fori_loop(0, chunks, one_chunk, 0)

    def finish(j, carry):
        @pl.when(has_up)
        def _():
            for copy in row_copies(j, True):
                copy.wait_send()

        @pl.when(has_down)
        def _():
            for copy in row_copies(j, False):
                copy.wait_send()

        return carry

    lax.fori_loop(0, chunks, finish, 0)


def to_trace(basis, spectrum):
    high = spectrum.astype(jnp.bfloat16)
    low = (spectrum - high.astype(jnp.float32)).astype(jnp.bfloat16)
    both = jnp.concatenate([high, low, high, low], axis=0)
    return jnp.dot(basis, both, preferred_element_type=jnp.float32)


def subtract_kernel(
    rows, width, m_ref, d_ref, basis_ref, p_ref, q_ref, shifted, power, data, residual, held
):
    nt = m_ref.shape[1]
    reach = filter_reach
    diameter = 2 * reach + 1
    samples = basis_ref.shape[0]
    turns = rows // 8
    basis = basis_ref[...]
    lane = lax.broadcasted_iota(jnp.int32, (8, 8, LANES), 2)

    def traces(ref, count, tiles):
        def four_rows(n, carry):
            spectrum = jnp.concatenate(
                [ref[4 * n + r, t].reshape(samples, LANES) for r in range(4) for t in tiles],
                axis=1,
            )
            found = to_trace(basis, spectrum)
            for r in range(4):
                for k in range(len(tiles)):
                    at = (r * len(tiles) + k) * LANES
                    held[k, 4 * n + r] = found[:, at : at + LANES]
            return carry

        lax.fori_loop(0, count // 4, four_rows, 0)

    def turned(k, q, at):
        return jnp.swapaxes(jnp.stack([held[k, turns * s + q, at, :] for s in range(8)]), 0, 1)

    def make(b):
        used = [
            t
            for t in range(nt)
            if STRIDE * (t + 1) - reach > LANES * b - reach
            and STRIDE * t - reach < LANES * (b + 1) + reach
        ]
        traces(m_ref, rows + 2 * reach, used)

        def one_vector(q, carry):
            def some_times(n, total):
                at = pl.ds(pl.multiple_of(8 * n, 8), 8)
                tiles = [-turned(k, q, at) for k in range(len(used))]
                for shift in range(diameter):
                    low = LANES * b + shift - reach
                    value = None
                    for t, tile in zip(used, tiles):
                        begin, end = STRIDE * t - reach, STRIDE * (t + 1) - reach
                        if end <= low or begin >= low + LANES:
                            continue
                        turn = (STRIDE * t - HALO - low) % LANES
                        moved = pltpu.roll(tile, turn, 2) if turn else tile
                        value = (
                            moved
                            if value is None
                            else jnp.where(lane < begin - low, value, moved)
                        )
                    shifted[q, shift, at] = value
                    total = total + jnp.sum(value * value, axis=0)
                return total

            power[q] = lax.fori_loop(
                0, samples // 8, some_times, jnp.zeros((8, LANES), jnp.float32)
            )
            return carry

        lax.fori_loop(0, turns + 2 * reach, one_vector, 0)
        traces(d_ref, rows, [b])

    for b in range(width // LANES):
        pl.when(pl.program_id(0) == b)(functools.partial(make, b))

    def turn_data(q, carry):
        for n in range(samples // 8):
            data[q, 8 * n : 8 * n + 8] = turned(0, q, slice(8 * n, 8 * n + 8))
        return carry

    lax.fori_loop(0, turns, turn_data, 0)

    taps = [(a, c) for a in range(diameter) for c in range(diameter)]
    together = 4

    def one_vector(q, carry):
        def tap(t, a, c):
            return shifted[q + a, c, t]

        energy = energy_floor
        for a in range(diameter):
            energy = energy + power[q + a]
        gain = step_size / energy

        def match(read):
            def some(n, sums):
                sums = list(sums)
                for u in range(together):
                    t = together * n + u
                    value = read(t)
                    sums = [sums[k] + value * tap(t, a, c) for k, (a, c) in enumerate(taps)]
                return tuple(sums)

            zero = jnp.zeros((8, LANES), jnp.float32)
            sums = lax.fori_loop(0, samples // together, some, (zero,) * len(taps))
            return [found * gain for found in sums]

        def remove(weights, write):
            def some(n, carry):
                for u in range(together):
                    t = together * n + u
                    parts = [None] * diameter
                    for weight, (a, c) in zip(weights, taps):
                        term = weight * tap(t, a, c)
                        parts[c] = term if parts[c] is None else parts[c] + term
                    filtered = functools.reduce(jnp.add, parts)
                    write(t, data[q, t] - filtered)
                return carry

            lax.fori_loop(0, samples // together, some, 0)

        def keep(t, value):
            residual[t] = value

        at = pl.ds(q, 8, stride=turns)

        def put(t, value):
            p_ref[t, at, :] = value
            q_ref[t, at, :] = tap(t, reach, reach)

        weights = match(lambda t: data[q, t])
        for repeat in range(1, PASSES):
            remove(weights, keep)
            weights = [w + more for w, more in zip(weights, match(lambda t: residual[t]))]
        remove(weights, put)
        return carry

    lax.fori_loop(0, turns, one_vector, 0)


def local(mesh_shape, data_spectrum, velocity_level):
    nz, tiles = mesh_shape["freq"], mesh_shape["tile"]
    _, local_freqs, rows, cols = data_spectrum.shape
    orders = local_freqs * nz
    samples = 2 * orders
    width = cols // nz
    per_chunk = 8 // nz
    chunks = local_freqs // per_chunk
    nt = tile_count(width)
    mains = width // LANES
    full = rows + 2 * HALO
    reach = filter_reach

    around = jnp.pad(data_spectrum, ((0, 0), (0, 0), (0, 0), (HALO, HALO)))
    strips = jnp.stack(
        [
            jnp.concatenate(
                [
                    around[..., d * width : d * width + HALO],
                    around[..., (d + 1) * width + HALO : (d + 1) * width + 2 * HALO],
                ],
                axis=-1,
            )
            for d in range(nz)
        ]
    )
    strips = strips.reshape(nz, 2, chunks, per_chunk, rows, 2 * HALO)
    strips = strips.transpose(0, 2, 4, 1, 3, 5).reshape(nz, chunks, rows, -1)
    strips = jnp.pad(strips, ((0, 0),) * 3 + ((0, LANES - strips.shape[-1]),))
    levels = jnp.pad(velocity_level, ((0, 0), (LANES, LANES)), constant_values=OUTSIDE)
    table = jnp.asarray(coefficient_table(orders, nz, per_chunk, chunks))
    basis = jnp.asarray(trace_basis(orders, nz, per_chunk, chunks))

    dma = pltpu.SemaphoreType.DMA
    vmem = pl.BlockSpec(memory_space=pltpu.VMEM)
    hbm = pl.BlockSpec(memory_space=pl.ANY)
    predicted, recorded = pl.pallas_call(
        functools.partial(predict_kernel, tiles, nz, per_chunk, chunks, rows, width),
        out_shape=(
            jax.ShapeDtypeStruct((rows + 8, nt, 2, chunks, 8, LANES), jnp.float32),
            jax.ShapeDtypeStruct((rows, mains, 2, chunks, 8, LANES), jnp.float32),
        ),
        in_specs=[hbm, hbm, hbm, vmem],
        out_specs=(vmem, vmem),
        scratch_shapes=[
            pltpu.VMEM((chunks, 2, 8, full, width), jnp.float32),
            pltpu.VMEM((chunks, nz, full, LANES), jnp.float32),
            pltpu.VMEM((full, width + 2 * LANES), jnp.int32),
            pltpu.VMEM((nt, full, 8, LANES), jnp.int32),
            pltpu.VMEM((4, nt, full + ROWS, 8, LANES), jnp.float32),
            pltpu.VMEM((2, nt, full + ROWS, 8, LANES), jnp.float32),
            pltpu.VMEM((2, nt, full + ROWS, 8, LANES), jnp.float32),
            dma((chunks, nz)), dma((chunks, nz)), dma((chunks, nz)), dma((chunks, nz)),
            dma((chunks, 2)), dma((chunks, 2)), dma((chunks, 2)), dma((chunks, 2)),
            dma((2,)), dma((2,)), dma((chunks + 1, 2)),
        ],
        compiler_params=pltpu.CompilerParams(
            collective_id=0, has_side_effects=True, vmem_limit_bytes=56 * 2**20
        ),
        name="predict",
    )(data_spectrum, strips, levels, table)

    block = pl.BlockSpec((samples, rows, LANES), lambda b: (0, 0, b))
    out = jax.ShapeDtypeStruct((samples, rows, width), jnp.float32)
    turns = rows // 8
    return pl.pallas_call(
        functools.partial(subtract_kernel, rows, width),
        grid=(mains,),
        out_shape=(out, out),
        in_specs=[vmem, vmem, vmem],
        out_specs=(block, block),
        scratch_shapes=[
            pltpu.VMEM((turns + 2 * reach, 2 * reach + 1, samples, 8, LANES), jnp.float32),
            pltpu.VMEM((turns + 2 * reach, 8, LANES), jnp.float32),
            pltpu.VMEM((turns, samples, 8, LANES), jnp.float32),
            pltpu.VMEM((samples, 8, LANES), jnp.float32),
            pltpu.VMEM((nt, rows + 2 * reach, samples, LANES), jnp.float32),
        ],
        compiler_params=pltpu.CompilerParams(vmem_limit_bytes=56 * 2**20),
        name="subtract",
    )(predicted, recorded, basis)


def solution(mesh):
    in_specs = (P(None, "freq", "tile", None), P("tile", None))
    out_specs = (P(None, "tile", "freq"), P(None, "tile", "freq"))
    return jax.shard_map(
        functools.partial(local, dict(mesh.shape)),
        mesh=mesh, in_specs=in_specs, out_specs=out_specs, check_vma=False,
    )
```

```python
import functools
import math

import jax
import jax.numpy as jnp
import ml_dtypes
import numpy as np
from jax import lax
from jax.experimental import pallas as pl
from jax.experimental.pallas import tpu as pltpu
from jax.sharding import PartitionSpec as P

GROUPS = 3
PASSES = 3
STEPS = 4 * GROUPS

damping = 0.2
paraxial_top = 0.1
depth_step = 10.0
cell_width = 12.5
step_size = 0.6
energy_floor = 1e-05
filter_reach = 2

HALO = 16
LANES = 128
ROWS = 12
PAIR = 2
STRIDE = 100
OUTSIDE = 127
MESH = pl.DeviceIdType.MESH


def tile_count(width):
    count = 1
    while STRIDE * count < width + filter_reach + 1:
        count += 1
    return count


def overlapped(pieces, tile, lane):
    origin = STRIDE * tile - HALO + LANES
    k, off = origin // LANES, origin % LANES
    turn = LANES - off
    axis = pieces[0].ndim - 1
    return jnp.where(
        lane < turn, pltpu.roll(pieces[k], turn, axis), pltpu.roll(pieces[k + 1], turn, axis)
    )


def coefficient_table(orders, nz, per_chunk, chunks):
    table = np.zeros((chunks, 4, 8, LANES), np.float64)
    velocity = 1500.0 + 250.0 * np.arange(OUTSIDE)
    for j in range(chunks):
        for s in range(nz):
            for i in range(per_chunk):
                k = s * (orders // nz) + j * per_chunk + i
                omega = 4.0 * math.pi * (k + 1)
                theta = omega * depth_step / velocity
                q = velocity / (omega * cell_width)
                spread = damping + 1j * paraxial_top * q / (1.0 + q)
                turn = np.exp(1j * theta)
                centre = turn * (1.0 - 4.0 * spread)
                beside = turn * spread
                table[j, :, s * per_chunk + i, :OUTSIDE] = np.stack(
                    [centre.real, centre.imag, beside.real, beside.imag]
                )
    return table.astype(np.float32)


def trace_basis(orders, nz, per_chunk, chunks):
    samples = 2 * orders
    times = np.arange(samples)[:, None] + 0.5
    order = [
        s * (orders // nz) + j * per_chunk + i
        for j in range(chunks)
        for s in range(nz)
        for i in range(per_chunk)
    ]
    angles = 2.0 * math.pi * (np.array(order)[None, :] + 1.0) * times / samples
    basis = np.concatenate([np.cos(angles), -np.sin(angles)], axis=1) / math.sqrt(orders)
    basis = basis.astype(np.float32)
    high = basis.astype(ml_dtypes.bfloat16)
    low = (basis - high.astype(np.float32)).astype(ml_dtypes.bfloat16)
    return np.concatenate([high, high, low], axis=1)


def predict_kernel(
    tiles, nz, per_chunk, chunks, rows, width,
    x_ref, strip_ref, level_ref, table_ref,
    m_ref, d_ref,
    ext, sext, lext, index, coef, state, other,
    a_send, a_recv, s_send, s_recv, r_send, r_recv, q_send, q_recv, l_send, l_recv, own,
):
    tile = lax.axis_index("tile")
    me = lax.axis_index("freq")
    has_up = tile > 0
    has_down = tile < tiles - 1
    nt = tile_count(width)
    mains = width // LANES
    full = rows + 2 * HALO
    inner = pl.ds(HALO, rows)
    window = pl.ds(pl.multiple_of(me * width, LANES), width + 2 * LANES)

    barrier = pltpu.get_barrier_semaphore()
    for hop in range(1, nz):
        pl.semaphore_signal(
            barrier, inc=1, device_id=(tile, lax.rem(me + hop, nz)), device_id_type=MESH
        )

    @pl.when(has_up)
    def _():
        pl.semaphore_signal(barrier, inc=1, device_id=(tile - 1, me), device_id_type=MESH)

    @pl.when(has_down)
    def _():
        pl.semaphore_signal(barrier, inc=1, device_id=(tile + 1, me), device_id_type=MESH)

    pl.semaphore_wait(
        barrier, nz - 1 + has_up.astype(jnp.int32) + has_down.astype(jnp.int32)
    )

    def level_copy(up):
        src = level_ref.at[pl.ds(0 if up else rows - HALO, HALO), window]
        dst = lext.at[pl.ds(HALO + rows if up else 0, HALO), :]
        way = 0 if up else 1
        return pltpu.make_async_remote_copy(
            src_ref=src, dst_ref=dst, send_sem=l_send.at[way], recv_sem=l_recv.at[way],
            device_id=(tile + (-1 if up else 1), me), device_id_type=MESH,
        )

    def main_copy(j, dest, source):
        return pltpu.make_async_remote_copy(
            src_ref=x_ref.at[
                :, pl.ds(j * per_chunk, per_chunk), :,
                pl.ds(pl.multiple_of(dest * width, LANES), width),
            ],
            dst_ref=ext.at[j, :, pl.ds(source * per_chunk, per_chunk), inner, :],
            send_sem=a_send.at[j, dest], recv_sem=a_recv.at[j, source],
            device_id=(tile, dest), device_id_type=MESH,
        )

    def strip_copy(j, dest, source):
        return pltpu.make_async_remote_copy(
            src_ref=strip_ref.at[dest, j],
            dst_ref=sext.at[j, source, inner, :],
            send_sem=s_send.at[j, dest], recv_sem=s_recv.at[j, source],
            device_id=(tile, dest), device_id_type=MESH,
        )

    def row_copies(j, up):
        src = pl.ds(HALO if up else rows, HALO)
        dst = pl.ds(HALO + rows if up else 0, HALO)
        way = 0 if up else 1
        target = (tile + (-1 if up else 1), me)
        return (
            pltpu.make_async_remote_copy(
                src_ref=ext.at[j, :, :, src, :], dst_ref=ext.at[j, :, :, dst, :],
                send_sem=r_send.at[j, way], recv_sem=r_recv.at[j, way],
                device_id=target, device_id_type=MESH,
            ),
            pltpu.make_async_remote_copy(
                src_ref=sext.at[j, :, src, :], dst_ref=sext.at[j, :, dst, :],
                send_sem=q_send.at[j, way], recv_sem=q_recv.at[j, way],
                device_id=target, device_id_type=MESH,
            ),
        )

    def own_copies(j):
        return (
            pltpu.make_async_copy(
                x_ref.at[
                    :, pl.ds(j * per_chunk, per_chunk), :,
                    pl.ds(pl.multiple_of(me * width, LANES), width),
                ],
                ext.at[j, :, pl.ds(me * per_chunk, per_chunk), inner, :],
                own.at[j, 0],
            ),
            pltpu.make_async_copy(
                strip_ref.at[me, j], sext.at[j, me, inner, :], own.at[j, 1]
            ),
        )

    own_level = pltpu.make_async_copy(
        level_ref.at[:, window], lext.at[inner, :], own.at[chunks, 0]
    )

    @pl.when(has_up)
    def _():
        level_copy(True).start()

    @pl.when(has_down)
    def _():
        level_copy(False).start()

    own_level.start()

    def send(j):
        for hop in range(1, nz):
            dest = lax.rem(me + hop, nz)
            strip_copy(j, dest, me).start()
            main_copy(j, dest, me).start()

    def sent(j):
        for hop in range(1, nz):
            dest = lax.rem(me + hop, nz)
            strip_copy(j, dest, me).wait_send()
            main_copy(j, dest, me).wait_send()

    send(0)

    def keep(j, carry):
        for copy in own_copies(j):
            copy.start()
        return carry

    lax.fori_loop(0, chunks, keep, 0)

    top, bottom = pl.ds(0, HALO), pl.ds(HALO + rows, HALO)
    for missing, edge in ((jnp.logical_not(has_up), top), (jnp.logical_not(has_down), bottom)):

        @pl.when(missing)
        def _(edge=edge):
            lext[edge, :] = jnp.full((HALO, lext.shape[1]), OUTSIDE, jnp.int32)

            def clear(j, carry):
                for part in range(2):
                    for f in range(8):
                        ext[j, part, f, edge, :] = jnp.zeros((HALO, width), jnp.float32)
                for s in range(nz):
                    sext[j, s, edge, :] = jnp.zeros((HALO, LANES), jnp.float32)
                return carry

            lax.fori_loop(0, chunks, clear, 0)

    own_level.wait()

    @pl.when(has_up)
    def _():
        level_copy(True).wait_send()
        level_copy(False).wait_recv()

    @pl.when(has_down)
    def _():
        level_copy(False).wait_send()
        level_copy(True).wait_recv()

    lane2 = lax.broadcasted_iota(jnp.int32, (8, LANES), 1)
    lane3 = lax.broadcasted_iota(jnp.int32, (8, 8, LANES), 2)

    def make_index(b, carry):
        at = pl.ds(pl.multiple_of(b * 8, 8), 8)
        pieces = [lext[at, k * LANES : (k + 1) * LANES] for k in range(mains + 2)]
        for t in range(nt):
            found = overlapped(pieces, t, lane2)
            index[t, at] = jnp.broadcast_to(found[:, None, :], (8, 8, LANES))
        return carry

    lax.fori_loop(0, full // 8, make_index, 0)

    def arrive(j):
        sent(j)

        @pl.when(j + 1 < chunks)
        def _():
            send(j + 1)

        for copy in own_copies(j):
            copy.wait()
        for hop in range(1, nz):
            source = lax.rem(me + hop, nz)
            main_copy(j, me, source).wait_recv()
            strip_copy(j, me, source).wait_recv()

        @pl.when(has_up)
        def _():
            for copy in row_copies(j, True):
                copy.start()

        @pl.when(has_down)
        def _():
            for copy in row_copies(j, False):
                copy.start()

    def make_coefs(j):
        def make_coef(b, carry):
            values = [table_ref[j, c] for c in range(4)]
            for r in range(8):
                for t in range(nt):
                    at = index[t, 8 * b + r]
                    for c in range(4):
                        coef[c, t, 8 * b + r] = jnp.take_along_axis(
                            values[c], at, axis=1, mode="promise_in_bounds"
                        )
            return carry

        lax.fori_loop(0, full // 8, make_coef, 0)

    make_coefs(0)
    arrive(0)

    def one_chunk(j, carry):
        pl.when(j > 0)(functools.partial(make_coefs, j))

        @pl.when(has_up)
        def _():
            for copy in row_copies(j, False):
                copy.wait_recv()

        @pl.when(has_down)
        def _():
            for copy in row_copies(j, True):
                copy.wait_recv()

        def fill(b, carry):
            at = pl.ds(pl.multiple_of(b * 8, 8), 8)
            for part in range(2):
                main = [
                    jnp.swapaxes(ext[j, part, :, at, k * LANES : (k + 1) * LANES], 0, 1)
                    for k in range(mains)
                ]
                strips = []
                for s in range(nz):
                    strip = sext[j, s, at, :]
                    for i in range(per_chunk):
                        base = (part * per_chunk + i) * 2 * HALO
                        strips.append(pltpu.roll(strip, (LANES - base - HALO) % LANES, 1))
                strip = jnp.swapaxes(jnp.stack(strips), 0, 1)
                pieces = [strip] + main + [strip]
                for t in range(nt):
                    state[part, t, at] = overlapped(pieces, t, lane3)

                @pl.when((b >= HALO // 8) & (b < (HALO + rows) // 8))
                def _():
                    for k in range(mains):
                        for r in range(8):
                            d_ref[b * 8 - HALO + r, k, part, j] = main[k][r]
            return carry

        lax.fori_loop(0, full // 8, fill, 0)

        def one_step(s, old, new):
            first = HALO - filter_reach - STEPS + s
            count = rows + 2 * (filter_reach + STEPS) - 2 * s

            def block(b, carry):
                e = first + ROWS * b

                def row(r):
                    return [(old[0, t, e + r], old[1, t, e + r]) for t in range(nt)]

                above, here = row(-1), row(0)
                for r in range(ROWS):
                    below = row(r + 1)
                    for t in range(nt):
                        p, q = here[t]
                        nr = (above[t][0] + below[t][0]) + (
                            pltpu.roll(p, 1, 1) + pltpu.roll(p, LANES - 1, 1)
                        )
                        ni = (above[t][1] + below[t][1]) + (
                            pltpu.roll(q, 1, 1) + pltpu.roll(q, LANES - 1, 1)
                        )
                        cr, ci = coef[0, t, e + r], coef[1, t, e + r]
                        br, bi = coef[2, t, e + r], coef[3, t, e + r]
                        new[0, t, e + r] = (cr * p - ci * q) + (br * nr - bi * ni)
                        new[1, t, e + r] = (cr * q + ci * p) + (br * ni + bi * nr)
                    above, here = here, below
                return carry

            lax.fori_loop(0, (count + ROWS - 1) // ROWS, block, 0)

        def two_steps(n, carry):
            @pl.when((n == STEPS // 2 - 1) & (j + 1 < chunks))
            def _():
                arrive(j + 1)

            one_step(2 * n + 1, state, other)
            one_step(2 * n + 2, other, state)
            return carry

        lax.fori_loop(0, STEPS // 2, two_steps, 0)

        def put(b, carry):
            for r in range(4):
                for t in range(nt):
                    for part in range(2):
                        m_ref[4 * b + r, t, part, j] = state[
                            part, t, 4 * b + r + HALO - filter_reach
                        ]
            return carry

        lax.fori_loop(0, (rows + 8) // 4, put, 0)
        return carry

    lax.fori_loop(0, chunks, one_chunk, 0)

    def finish(j, carry):
        @pl.when(has_up)
        def _():
            for copy in row_copies(j, True):
                copy.wait_send()

        @pl.when(has_down)
        def _():
            for copy in row_copies(j, False):
                copy.wait_send()

        return carry

    lax.fori_loop(0, chunks, finish, 0)


def to_trace(basis, spectrum):
    high = spectrum.astype(jnp.bfloat16)
    low = (spectrum - high.astype(jnp.float32)).astype(jnp.bfloat16)
    both = jnp.concatenate([high, low, high], axis=0)
    return jnp.dot(basis, both, preferred_element_type=jnp.float32)


def subtract_kernel(
    rows, width, m_ref, d_ref, basis_ref, p_ref, q_ref, shifted, power, data, residual, held
):
    nt = m_ref.shape[1]
    reach = filter_reach
    diameter = 2 * reach + 1
    samples = basis_ref.shape[0]
    turns = rows // 8
    basis = basis_ref[...]
    lane = lax.broadcasted_iota(jnp.int32, (8, 8, LANES), 2)

    def traces(ref, count, tiles):
        def four_rows(n, carry):
            spectrum = jnp.concatenate(
                [ref[4 * n + r, t].reshape(samples, LANES) for r in range(4) for t in tiles],
                axis=1,
            )
            found = to_trace(basis, spectrum)
            for r in range(4):
                for k in range(len(tiles)):
                    at = (r * len(tiles) + k) * LANES
                    held[k, 4 * n + r] = found[:, at : at + LANES]
            return carry

        lax.fori_loop(0, count // 4, four_rows, 0)

    def turned(k, q, at):
        return jnp.swapaxes(jnp.stack([held[k, turns * s + q, at, :] for s in range(8)]), 0, 1)

    def make(b):
        used = [
            t
            for t in range(nt)
            if STRIDE * (t + 1) - reach > LANES * b - reach
            and STRIDE * t - reach < LANES * (b + 1) + reach
        ]
        traces(m_ref, rows + 2 * reach, used)

        def one_vector(q, carry):
            def some_times(n, total):
                at = pl.ds(pl.multiple_of(8 * n, 8), 8)
                tiles = [-turned(k, q, at) for k in range(len(used))]
                for shift in range(diameter):
                    low = LANES * b + shift - reach
                    value = None
                    for t, tile in zip(used, tiles):
                        begin, end = STRIDE * t - reach, STRIDE * (t + 1) - reach
                        if end <= low or begin >= low + LANES:
                            continue
                        turn = (STRIDE * t - HALO - low) % LANES
                        moved = pltpu.roll(tile, turn, 2) if turn else tile
                        value = (
                            moved
                            if value is None
                            else jnp.where(lane < begin - low, value, moved)
                        )
                    shifted[q, shift, at] = value
                    total = total + jnp.sum(value * value, axis=0)
                return total

            power[q] = lax.fori_loop(
                0, samples // 8, some_times, jnp.zeros((8, LANES), jnp.float32)
            )
            return carry

        lax.fori_loop(0, turns + 2 * reach, one_vector, 0)
        traces(d_ref, rows, [b])

    for b in range(width // LANES):
        pl.when(pl.program_id(0) == b)(functools.partial(make, b))

    def turn_data(q, carry):
        for n in range(samples // 8):
            data[q, 8 * n : 8 * n + 8] = turned(0, q, slice(8 * n, 8 * n + 8))
        return carry

    lax.fori_loop(0, turns, turn_data, 0)

    taps = [(a, c) for a in range(diameter) for c in range(diameter)]
    zero = jnp.zeros((8, LANES), jnp.float32)

    def vector_pair(n, carry):
        first = PAIR * n
        pair = range(PAIR)

        def column(t, c):
            return [shifted[first + a, c, t] for a in range(diameter + PAIR - 1)]

        gains = []
        for v in pair:
            energy = energy_floor
            for a in range(diameter):
                energy = energy + power[first + v + a]
            gains.append(step_size / energy)

        def match(read):
            def some(t, sums):
                values = [read(v, t) for v in pair]
                sums = [list(part) for part in sums]
                for c in range(diameter):
                    cells = column(t, c)
                    for a in range(diameter):
                        for v in pair:
                            k = a * diameter + c
                            sums[v][k] = sums[v][k] + values[v] * cells[v + a]
                return tuple(tuple(part) for part in sums)

            sums = lax.fori_loop(0, samples, some, ((zero,) * len(taps),) * PAIR, unroll=2)
            return [[found * gains[v] for found in sums[v]] for v in pair]

        def remove(weights, write):
            def some(t, carry):
                filtered = [None] * PAIR
                for c in range(diameter):
                    cells = column(t, c)
                    for v in pair:
                        part = weights[v][c] * cells[v]
                        for a in range(1, diameter):
                            part = part + weights[v][a * diameter + c] * cells[v + a]
                        filtered[v] = part if c == 0 else filtered[v] + part
                for v in pair:
                    write(v, t, data[first + v, t] - filtered[v])
                return carry

            lax.fori_loop(0, samples, some, 0, unroll=2)

        def keep(v, t, value):
            residual[v, t] = value

        def put(v, t, value):
            at = pl.ds(first + v, 8, stride=turns)
            p_ref[t, at, :] = value
            q_ref[t, at, :] = shifted[first + v + reach, reach, t]

        weights = match(lambda v, t: data[first + v, t])
        for repeat in range(1, PASSES):
            remove(weights, keep)
            change = match(lambda v, t: residual[v, t])
            weights = [
                [w + more for w, more in zip(weights[v], change[v])] for v in pair
            ]
        remove(weights, put)
        return carry

    lax.fori_loop(0, turns // PAIR, vector_pair, 0)


def local(mesh_shape, data_spectrum, velocity_level):
    nz, tiles = mesh_shape["freq"], mesh_shape["tile"]
    _, local_freqs, rows, cols = data_spectrum.shape
    orders = local_freqs * nz
    samples = 2 * orders
    width = cols // nz
    per_chunk = 8 // nz
    chunks = local_freqs // per_chunk
    nt = tile_count(width)
    mains = width // LANES
    full = rows + 2 * HALO
    reach = filter_reach

    around = jnp.pad(data_spectrum, ((0, 0), (0, 0), (0, 0), (HALO, HALO)))
    strips = jnp.stack(
        [
            jnp.concatenate(
                [
                    around[..., d * width : d * width + HALO],
                    around[..., (d + 1) * width + HALO : (d + 1) * width + 2 * HALO],
                ],
                axis=-1,
            )
            for d in range(nz)
        ]
    )
    strips = strips.reshape(nz, 2, chunks, per_chunk, rows, 2 * HALO)
    strips = strips.transpose(0, 2, 4, 1, 3, 5).reshape(nz, chunks, rows, -1)
    strips = jnp.pad(strips, ((0, 0),) * 3 + ((0, LANES - strips.shape[-1]),))
    levels = jnp.pad(velocity_level, ((0, 0), (LANES, LANES)), constant_values=OUTSIDE)
    table = jnp.asarray(coefficient_table(orders, nz, per_chunk, chunks))
    basis = jnp.asarray(trace_basis(orders, nz, per_chunk, chunks))

    dma = pltpu.SemaphoreType.DMA
    vmem = pl.BlockSpec(memory_space=pltpu.VMEM)
    hbm = pl.BlockSpec(memory_space=pl.ANY)
    predicted, recorded = pl.pallas_call(
        functools.partial(predict_kernel, tiles, nz, per_chunk, chunks, rows, width),
        out_shape=(
            jax.ShapeDtypeStruct((rows + 8, nt, 2, chunks, 8, LANES), jnp.float32),
            jax.ShapeDtypeStruct((rows, mains, 2, chunks, 8, LANES), jnp.float32),
        ),
        in_specs=[hbm, hbm, hbm, vmem],
        out_specs=(vmem, vmem),
        scratch_shapes=[
            pltpu.VMEM((chunks, 2, 8, full, width), jnp.float32),
            pltpu.VMEM((chunks, nz, full, LANES), jnp.float32),
            pltpu.VMEM((full, width + 2 * LANES), jnp.int32),
            pltpu.VMEM((nt, full, 8, LANES), jnp.int32),
            pltpu.VMEM((4, nt, full + ROWS, 8, LANES), jnp.float32),
            pltpu.VMEM((2, nt, full + ROWS, 8, LANES), jnp.float32),
            pltpu.VMEM((2, nt, full + ROWS, 8, LANES), jnp.float32),
            dma((chunks, nz)), dma((chunks, nz)), dma((chunks, nz)), dma((chunks, nz)),
            dma((chunks, 2)), dma((chunks, 2)), dma((chunks, 2)), dma((chunks, 2)),
            dma((2,)), dma((2,)), dma((chunks + 1, 2)),
        ],
        compiler_params=pltpu.CompilerParams(
            collective_id=0, has_side_effects=True, vmem_limit_bytes=56 * 2**20
        ),
        name="predict",
    )(data_spectrum, strips, levels, table)

    block = pl.BlockSpec((samples, rows, LANES), lambda b: (0, 0, b))
    out = jax.ShapeDtypeStruct((samples, rows, width), jnp.float32)
    turns = rows // 8
    return pl.pallas_call(
        functools.partial(subtract_kernel, rows, width),
        grid=(mains,),
        out_shape=(out, out),
        in_specs=[vmem, vmem, vmem],
        out_specs=(block, block),
        scratch_shapes=[
            pltpu.VMEM((turns + 2 * reach, 2 * reach + 1, samples, 8, LANES), jnp.float32),
            pltpu.VMEM((turns + 2 * reach, 8, LANES), jnp.float32),
            pltpu.VMEM((turns, samples, 8, LANES), jnp.float32),
            pltpu.VMEM((PAIR, samples, 8, LANES), jnp.float32),
            pltpu.VMEM((nt, rows + 2 * reach, samples, LANES), jnp.float32),
        ],
        compiler_params=pltpu.CompilerParams(vmem_limit_bytes=56 * 2**20),
        name="subtract",
    )(predicted, recorded, basis)


def solution(mesh):
    in_specs = (P(None, "freq", "tile", None), P("tile", None))
    out_specs = (P(None, "tile", "freq"), P(None, "tile", "freq"))
    return jax.shard_map(
        functools.partial(local, dict(mesh.shape)),
        mesh=mesh, in_specs=in_specs, out_specs=out_specs, check_vma=False,
    )
```

```python
import functools
import math

import jax
import jax.numpy as jnp
import ml_dtypes
import numpy as np
from jax import lax
from jax.experimental import pallas as pl
from jax.experimental.pallas import tpu as pltpu
from jax.sharding import PartitionSpec as P

GROUPS = 3
PASSES = 3
STEPS = 4 * GROUPS

damping = 0.2
paraxial_top = 0.1
depth_step = 10.0
cell_width = 12.5
step_size = 0.6
energy_floor = 1e-05
filter_reach = 2

HALO = 16
LANES = 128
ROWS = 12
TOGETHER = 4
STRIDE = 100
OUTSIDE = 127
MESH = pl.DeviceIdType.MESH


def tile_count(width):
    count = 1
    while STRIDE * count < width + filter_reach + 1:
        count += 1
    return count


def overlapped(pieces, tile, lane):
    origin = STRIDE * tile - HALO + LANES
    k, off = origin // LANES, origin % LANES
    turn = LANES - off
    axis = pieces[0].ndim - 1
    return jnp.where(
        lane < turn, pltpu.roll(pieces[k], turn, axis), pltpu.roll(pieces[k + 1], turn, axis)
    )


def coefficient_table(orders, nz, per_chunk, chunks):
    table = np.zeros((chunks, 4, 8, LANES), np.float64)
    velocity = 1500.0 + 250.0 * np.arange(OUTSIDE)
    for j in range(chunks):
        for s in range(nz):
            for i in range(per_chunk):
                k = s * (orders // nz) + j * per_chunk + i
                omega = 4.0 * math.pi * (k + 1)
                theta = omega * depth_step / velocity
                q = velocity / (omega * cell_width)
                spread = damping + 1j * paraxial_top * q / (1.0 + q)
                turn = np.exp(1j * theta)
                centre = turn * (1.0 - 4.0 * spread)
                beside = turn * spread
                table[j, :, s * per_chunk + i, :OUTSIDE] = np.stack(
                    [centre.real, centre.imag, beside.real, beside.imag]
                )
    return table.astype(np.float32)


def trace_basis(orders, nz, per_chunk, chunks):
    samples = 2 * orders
    times = np.arange(samples)[:, None] + 0.5
    order = [
        s * (orders // nz) + j * per_chunk + i
        for j in range(chunks)
        for s in range(nz)
        for i in range(per_chunk)
    ]
    angles = 2.0 * math.pi * (np.array(order)[None, :] + 1.0) * times / samples
    basis = np.concatenate([np.cos(angles), -np.sin(angles)], axis=1) / math.sqrt(orders)
    basis = basis.astype(np.float32)
    high = basis.astype(ml_dtypes.bfloat16)
    low = (basis - high.astype(np.float32)).astype(ml_dtypes.bfloat16)
    return np.concatenate([high, high, low], axis=1)


def predict_kernel(
    tiles, nz, per_chunk, chunks, rows, width,
    x_ref, strip_ref, level_ref, table_ref,
    m_ref, d_ref,
    ext, sext, lext, index, coef, state, other,
    a_send, a_recv, s_send, s_recv, r_send, r_recv, q_send, q_recv, l_send, l_recv, own,
):
    tile = lax.axis_index("tile")
    me = lax.axis_index("freq")
    has_up = tile > 0
    has_down = tile < tiles - 1
    nt = tile_count(width)
    mains = width // LANES
    full = rows + 2 * HALO
    inner = pl.ds(HALO, rows)
    window = pl.ds(pl.multiple_of(me * width, LANES), width + 2 * LANES)

    barrier = pltpu.get_barrier_semaphore()
    for hop in range(1, nz):
        pl.semaphore_signal(
            barrier, inc=1, device_id=(tile, lax.rem(me + hop, nz)), device_id_type=MESH
        )

    @pl.when(has_up)
    def _():
        pl.semaphore_signal(barrier, inc=1, device_id=(tile - 1, me), device_id_type=MESH)

    @pl.when(has_down)
    def _():
        pl.semaphore_signal(barrier, inc=1, device_id=(tile + 1, me), device_id_type=MESH)

    pl.semaphore_wait(
        barrier, nz - 1 + has_up.astype(jnp.int32) + has_down.astype(jnp.int32)
    )

    def level_copy(up):
        src = level_ref.at[pl.ds(0 if up else rows - HALO, HALO), window]
        dst = lext.at[pl.ds(HALO + rows if up else 0, HALO), :]
        way = 0 if up else 1
        return pltpu.make_async_remote_copy(
            src_ref=src, dst_ref=dst, send_sem=l_send.at[way], recv_sem=l_recv.at[way],
            device_id=(tile + (-1 if up else 1), me), device_id_type=MESH,
        )

    def main_copy(j, dest, source):
        return pltpu.make_async_remote_copy(
            src_ref=x_ref.at[
                :, pl.ds(j * per_chunk, per_chunk), :,
                pl.ds(pl.multiple_of(dest * width, LANES), width),
            ],
            dst_ref=ext.at[j, :, pl.ds(source * per_chunk, per_chunk), inner, :],
            send_sem=a_send.at[j, dest], recv_sem=a_recv.at[j, source],
            device_id=(tile, dest), device_id_type=MESH,
        )

    def strip_copy(j, dest, source):
        return pltpu.make_async_remote_copy(
            src_ref=strip_ref.at[dest, j],
            dst_ref=sext.at[j, source, inner, :],
            send_sem=s_send.at[j, dest], recv_sem=s_recv.at[j, source],
            device_id=(tile, dest), device_id_type=MESH,
        )

    def row_copies(j, up):
        src = pl.ds(HALO if up else rows, HALO)
        dst = pl.ds(HALO + rows if up else 0, HALO)
        way = 0 if up else 1
        target = (tile + (-1 if up else 1), me)
        return (
            pltpu.make_async_remote_copy(
                src_ref=ext.at[j, :, :, src, :], dst_ref=ext.at[j, :, :, dst, :],
                send_sem=r_send.at[j, way], recv_sem=r_recv.at[j, way],
                device_id=target, device_id_type=MESH,
            ),
            pltpu.make_async_remote_copy(
                src_ref=sext.at[j, :, src, :], dst_ref=sext.at[j, :, dst, :],
                send_sem=q_send.at[j, way], recv_sem=q_recv.at[j, way],
                device_id=target, device_id_type=MESH,
            ),
        )

    def own_copies(j):
        return (
            pltpu.make_async_copy(
                x_ref.at[
                    :, pl.ds(j * per_chunk, per_chunk), :,
                    pl.ds(pl.multiple_of(me * width, LANES), width),
                ],
                ext.at[j, :, pl.ds(me * per_chunk, per_chunk), inner, :],
                own.at[j, 0],
            ),
            pltpu.make_async_copy(
                strip_ref.at[me, j], sext.at[j, me, inner, :], own.at[j, 1]
            ),
        )

    own_level = pltpu.make_async_copy(
        level_ref.at[:, window], lext.at[inner, :], own.at[chunks, 0]
    )

    @pl.when(has_up)
    def _():
        level_copy(True).start()

    @pl.when(has_down)
    def _():
        level_copy(False).start()

    own_level.start()

    def send(j):
        for hop in range(1, nz):
            dest = lax.rem(me + hop, nz)
            strip_copy(j, dest, me).start()
            main_copy(j, dest, me).start()

    def sent(j):
        for hop in range(1, nz):
            dest = lax.rem(me + hop, nz)
            strip_copy(j, dest, me).wait_send()
            main_copy(j, dest, me).wait_send()

    send(0)

    def keep(j, carry):
        for copy in own_copies(j):
            copy.start()
        return carry

    lax.fori_loop(0, chunks, keep, 0)

    top, bottom = pl.ds(0, HALO), pl.ds(HALO + rows, HALO)
    for missing, edge in ((jnp.logical_not(has_up), top), (jnp.logical_not(has_down), bottom)):

        @pl.when(missing)
        def _(edge=edge):
            lext[edge, :] = jnp.full((HALO, lext.shape[1]), OUTSIDE, jnp.int32)

            def clear(j, carry):
                for part in range(2):
                    for f in range(8):
                        ext[j, part, f, edge, :] = jnp.zeros((HALO, width), jnp.float32)
                for s in range(nz):
                    sext[j, s, edge, :] = jnp.zeros((HALO, LANES), jnp.float32)
                return carry

            lax.fori_loop(0, chunks, clear, 0)

    own_level.wait()

    @pl.when(has_up)
    def _():
        level_copy(True).wait_send()
        level_copy(False).wait_recv()

    @pl.when(has_down)
    def _():
        level_copy(False).wait_send()
        level_copy(True).wait_recv()

    lane2 = lax.broadcasted_iota(jnp.int32, (8, LANES), 1)
    lane3 = lax.broadcasted_iota(jnp.int32, (8, 8, LANES), 2)

    def make_index(b, carry):
        at = pl.ds(pl.multiple_of(b * 8, 8), 8)
        pieces = [lext[at, k * LANES : (k + 1) * LANES] for k in range(mains + 2)]
        for t in range(nt):
            found = overlapped(pieces, t, lane2)
            index[t, at] = jnp.broadcast_to(found[:, None, :], (8, 8, LANES))
        return carry

    lax.fori_loop(0, full // 8, make_index, 0)

    def arrive(j):
        sent(j)

        @pl.when(j + 1 < chunks)
        def _():
            send(j + 1)

        for copy in own_copies(j):
            copy.wait()
        for hop in range(1, nz):
            source = lax.rem(me + hop, nz)
            main_copy(j, me, source).wait_recv()
            strip_copy(j, me, source).wait_recv()

        @pl.when(has_up)
        def _():
            for copy in row_copies(j, True):
                copy.start()

        @pl.when(has_down)
        def _():
            for copy in row_copies(j, False):
                copy.start()

    arrive(0)

    def one_chunk(j, carry):
        def make_coef(b, carry):
            values = [table_ref[j, c] for c in range(4)]
            for r in range(8):
                for t in range(nt):
                    at = index[t, 8 * b + r]
                    for c in range(4):
                        coef[c, t, 8 * b + r] = jnp.take_along_axis(
                            values[c], at, axis=1, mode="promise_in_bounds"
                        )
            return carry

        lax.fori_loop(0, full // 8, make_coef, 0)

        @pl.when(has_up)
        def _():
            for copy in row_copies(j, False):
                copy.wait_recv()

        @pl.when(has_down)
        def _():
            for copy in row_copies(j, True):
                copy.wait_recv()

        def fill(b, carry):
            at = pl.ds(pl.multiple_of(b * 8, 8), 8)
            for part in range(2):
                main = [
                    jnp.swapaxes(ext[j, part, :, at, k * LANES : (k + 1) * LANES], 0, 1)
                    for k in range(mains)
                ]
                strips = []
                for s in range(nz):
                    strip = sext[j, s, at, :]
                    for i in range(per_chunk):
                        base = (part * per_chunk + i) * 2 * HALO
                        strips.append(pltpu.roll(strip, (LANES - base - HALO) % LANES, 1))
                strip = jnp.swapaxes(jnp.stack(strips), 0, 1)
                pieces = [strip] + main + [strip]
                for t in range(nt):
                    state[part, t, at] = overlapped(pieces, t, lane3)

                @pl.when((b >= HALO // 8) & (b < (HALO + rows) // 8))
                def _():
                    for k in range(mains):
                        for r in range(8):
                            d_ref[b * 8 - HALO + r, k, part, j] = main[k][r]
            return carry

        lax.fori_loop(0, full // 8, fill, 0)

        def one_step(s, old, new):
            first = HALO - filter_reach - STEPS + s
            count = rows + 2 * (filter_reach + STEPS) - 2 * s

            def block(b, carry):
                e = first + ROWS * b

                def row(r):
                    return [(old[0, t, e + r], old[1, t, e + r]) for t in range(nt)]

                above, here = row(-1), row(0)
                for r in range(ROWS):
                    below = row(r + 1)
                    for t in range(nt):
                        p, q = here[t]
                        nr = (above[t][0] + below[t][0]) + (
                            pltpu.roll(p, 1, 1) + pltpu.roll(p, LANES - 1, 1)
                        )
                        ni = (above[t][1] + below[t][1]) + (
                            pltpu.roll(q, 1, 1) + pltpu.roll(q, LANES - 1, 1)
                        )
                        cr, ci = coef[0, t, e + r], coef[1, t, e + r]
                        br, bi = coef[2, t, e + r], coef[3, t, e + r]
                        new[0, t, e + r] = (cr * p - ci * q) + (br * nr - bi * ni)
                        new[1, t, e + r] = (cr * q + ci * p) + (br * ni + bi * nr)
                    above, here = here, below
                return carry

            lax.fori_loop(0, (count + ROWS - 1) // ROWS, block, 0)

        def two_steps(n, carry):
            @pl.when((n == STEPS // 2 - 1) & (j + 1 < chunks))
            def _():
                arrive(j + 1)

            one_step(2 * n + 1, state, other)
            one_step(2 * n + 2, other, state)
            return carry

        lax.fori_loop(0, STEPS // 2, two_steps, 0)

        def put(b, carry):
            for r in range(4):
                for t in range(nt):
                    for part in range(2):
                        m_ref[4 * b + r, t, part, j] = state[
                            part, t, 4 * b + r + HALO - filter_reach
                        ]
            return carry

        lax.fori_loop(0, (rows + 8) // 4, put, 0)
        return carry

    lax.fori_loop(0, chunks, one_chunk, 0)

    def finish(j, carry):
        @pl.when(has_up)
        def _():
            for copy in row_copies(j, True):
                copy.wait_send()

        @pl.when(has_down)
        def _():
            for copy in row_copies(j, False):
                copy.wait_send()

        return carry

    lax.fori_loop(0, chunks, finish, 0)


def to_trace(basis, spectrum):
    high = spectrum.astype(jnp.bfloat16)
    low = (spectrum - high.astype(jnp.float32)).astype(jnp.bfloat16)
    both = jnp.concatenate([high, low, high], axis=0)
    return jnp.dot(basis, both, preferred_element_type=jnp.float32)


def subtract_kernel(
    rows, width, m_ref, d_ref, basis_ref, p_ref, q_ref, shifted, power, data, result
):
    i = pl.program_id(0)
    mains = width // LANES
    nt = m_ref.shape[1]
    reach = filter_reach
    diameter = 2 * reach + 1
    samples = basis_ref.shape[0]
    basis = basis_ref[...]
    lane = lax.broadcasted_iota(jnp.int32, (samples, LANES), 1)

    def traces(ref, first, count):
        spectrum = jnp.concatenate(
            [
                ref[first + r, t].reshape(samples, LANES)
                for r in range(TOGETHER)
                for t in range(count)
            ],
            axis=1,
        )
        found = to_trace(basis, spectrum)
        return [
            [
                found[:, (r * count + t) * LANES : (r * count + t + 1) * LANES]
                for t in range(count)
            ]
            for r in range(TOGETHER)
        ]

    def make_rows(n, carry):
        for r, tiles in enumerate(traces(m_ref, TOGETHER * n, nt)):
            row = TOGETHER * n + r
            for b in range(mains):
                total = None
                for shift in range(diameter):
                    low = LANES * b + shift - reach
                    value = None
                    for t in range(nt):
                        begin, end = STRIDE * t - reach, STRIDE * (t + 1) - reach
                        if end <= low or begin >= low + LANES:
                            continue
                        turn = (STRIDE * t - HALO - low) % LANES
                        moved = pltpu.roll(tiles[t], turn, 1) if turn else tiles[t]
                        value = (
                            moved
                            if value is None
                            else jnp.where(lane < begin - low, value, moved)
                        )
                    value = -value
                    shifted[shift, b, row] = value
                    part = jnp.sum((value * value).reshape(samples // 8, 8, LANES), axis=0)
                    total = part if total is None else total + part
                power[b, row] = total
        return carry

    lax.fori_loop(
        jnp.where(i == 0, 0, (8 * i + 2 * reach) // TOGETHER),
        (8 * i + 8 + 2 * reach) // TOGETHER,
        make_rows,
        0,
    )

    def make_data(n, carry):
        for r, tiles in enumerate(traces(d_ref, 8 * i + TOGETHER * n, mains)):
            for b in range(mains):
                data[b, TOGETHER * n + r] = tiles[b]
        return carry

    lax.fori_loop(0, 8 // TOGETHER, make_data, 0)

    taps = [(a, c) for a in range(diameter) for c in range(diameter)]

    def total(values):
        return jnp.sum(values, axis=0, keepdims=True)

    def one_row(n, carry):
        r, b = n // mains, lax.rem(n, mains)

        def tap(a, c):
            return shifted[c, b, 8 * i + r + a]

        recorded = data[b, r]
        energy = power[b, 8 * i + r]
        for a in range(1, diameter):
            energy = energy + power[b, 8 * i + r + a]
        gain = step_size / (energy_floor + total(energy))

        def remove(weights):
            residual = recorded
            for weight, (a, c) in zip(weights, taps):
                residual = residual - weight * tap(a, c)
            return residual

        weights = [total(recorded * tap(a, c)) * gain for a, c in taps]
        for repeat in range(1, PASSES):
            residual = remove(weights)
            weights = [
                w + total(residual * tap(a, c)) * gain for w, (a, c) in zip(weights, taps)
            ]
        result[b, r] = remove(weights)
        return carry

    lax.fori_loop(0, 8 * mains, one_row, 0)

    for b in range(mains):
        at = slice(b * LANES, (b + 1) * LANES)
        for k in range(samples // 8):
            part = slice(8 * k, 8 * k + 8)
            p_ref[part, :, at] = jnp.swapaxes(result[b, :, part, :], 0, 1)
            q_ref[part, :, at] = jnp.swapaxes(
                shifted[reach, b, pl.ds(8 * i + reach, 8), part, :], 0, 1
            )


def local(mesh_shape, data_spectrum, velocity_level):
    nz, tiles = mesh_shape["freq"], mesh_shape["tile"]
    _, local_freqs, rows, cols = data_spectrum.shape
    orders = local_freqs * nz
    samples = 2 * orders
    width = cols // nz
    per_chunk = 8 // nz
    chunks = local_freqs // per_chunk
    nt = tile_count(width)
    mains = width // LANES
    full = rows + 2 * HALO
    reach = filter_reach

    around = jnp.pad(data_spectrum, ((0, 0), (0, 0), (0, 0), (HALO, HALO)))
    strips = jnp.stack(
        [
            jnp.concatenate(
                [
                    around[..., d * width : d * width + HALO],
                    around[..., (d + 1) * width + HALO : (d + 1) * width + 2 * HALO],
                ],
                axis=-1,
            )
            for d in range(nz)
        ]
    )
    strips = strips.reshape(nz, 2, chunks, per_chunk, rows, 2 * HALO)
    strips = strips.transpose(0, 2, 4, 1, 3, 5).reshape(nz, chunks, rows, -1)
    strips = jnp.pad(strips, ((0, 0),) * 3 + ((0, LANES - strips.shape[-1]),))
    levels = jnp.pad(velocity_level, ((0, 0), (LANES, LANES)), constant_values=OUTSIDE)
    table = jnp.asarray(coefficient_table(orders, nz, per_chunk, chunks))
    basis = jnp.asarray(trace_basis(orders, nz, per_chunk, chunks))

    dma = pltpu.SemaphoreType.DMA
    vmem = pl.BlockSpec(memory_space=pltpu.VMEM)
    hbm = pl.BlockSpec(memory_space=pl.ANY)
    predicted, recorded = pl.pallas_call(
        functools.partial(predict_kernel, tiles, nz, per_chunk, chunks, rows, width),
        out_shape=(
            jax.ShapeDtypeStruct((rows + 8, nt, 2, chunks, 8, LANES), jnp.float32),
            jax.ShapeDtypeStruct((rows, mains, 2, chunks, 8, LANES), jnp.float32),
        ),
        in_specs=[hbm, hbm, hbm, vmem],
        out_specs=(vmem, vmem),
        scratch_shapes=[
            pltpu.VMEM((chunks, 2, 8, full, width), jnp.float32),
            pltpu.VMEM((chunks, nz, full, LANES), jnp.float32),
            pltpu.VMEM((full, width + 2 * LANES), jnp.int32),
            pltpu.VMEM((nt, full, 8, LANES), jnp.int32),
            pltpu.VMEM((4, nt, full + ROWS, 8, LANES), jnp.float32),
            pltpu.VMEM((2, nt, full + ROWS, 8, LANES), jnp.float32),
            pltpu.VMEM((2, nt, full + ROWS, 8, LANES), jnp.float32),
            dma((chunks, nz)), dma((chunks, nz)), dma((chunks, nz)), dma((chunks, nz)),
            dma((chunks, 2)), dma((chunks, 2)), dma((chunks, 2)), dma((chunks, 2)),
            dma((2,)), dma((2,)), dma((chunks + 1, 2)),
        ],
        compiler_params=pltpu.CompilerParams(
            collective_id=0, has_side_effects=True, vmem_limit_bytes=56 * 2**20
        ),
        name="predict",
    )(data_spectrum, strips, levels, table)

    block = pl.BlockSpec((samples, 8, width), lambda i: (0, i, 0))
    out = jax.ShapeDtypeStruct((samples, rows, width), jnp.float32)
    return pl.pallas_call(
        functools.partial(subtract_kernel, rows, width),
        grid=(rows // 8,),
        out_shape=(out, out),
        in_specs=[vmem, vmem, vmem],
        out_specs=(block, block),
        scratch_shapes=[
            pltpu.VMEM((2 * reach + 1, mains, rows + 2 * reach, samples, LANES), jnp.float32),
            pltpu.VMEM((mains, rows + 2 * reach, 8, LANES), jnp.float32),
            pltpu.VMEM((mains, 8, samples, LANES), jnp.float32),
            pltpu.VMEM((mains, 8, samples, LANES), jnp.float32),
        ],
        compiler_params=pltpu.CompilerParams(vmem_limit_bytes=56 * 2**20),
        name="subtract",
    )(predicted, recorded, basis)


def solution(mesh):
    in_specs = (P(None, "freq", "tile", None), P("tile", None))
    out_specs = (P(None, "tile", "freq"), P(None, "tile", "freq"))
    return jax.shard_map(
        functools.partial(local, dict(mesh.shape)),
        mesh=mesh, in_specs=in_specs, out_specs=out_specs, check_vma=False,
    )
```

```python
import functools
import math

import jax
import jax.numpy as jnp
import ml_dtypes
import numpy as np
from jax import lax
from jax.experimental import pallas as pl
from jax.experimental.pallas import tpu as pltpu
from jax.sharding import PartitionSpec as P

GROUPS = 3
PASSES = 3
STEPS = 4 * GROUPS

damping = 0.2
paraxial_top = 0.1
depth_step = 10.0
cell_width = 12.5
step_size = 0.6
energy_floor = 1e-05
filter_reach = 2

HALO = 16
LANES = 128
ROWS = 16
TOGETHER = 4
STRIDE = 100
OUTSIDE = 127
MESH = pl.DeviceIdType.MESH


def tile_count(width):
    count = 1
    while STRIDE * count < width + filter_reach + 1:
        count += 1
    return count


def overlapped(pieces, tile, lane):
    origin = STRIDE * tile - HALO + LANES
    k, off = origin // LANES, origin % LANES
    turn = LANES - off
    axis = pieces[0].ndim - 1
    return jnp.where(
        lane < turn, pltpu.roll(pieces[k], turn, axis), pltpu.roll(pieces[k + 1], turn, axis)
    )


def coefficient_table(orders, nz, per_chunk, chunks):
    table = np.zeros((chunks, 4, 8, LANES), np.float64)
    velocity = 1500.0 + 250.0 * np.arange(OUTSIDE)
    for j in range(chunks):
        for s in range(nz):
            for i in range(per_chunk):
                k = s * (orders // nz) + j * per_chunk + i
                omega = 4.0 * math.pi * (k + 1)
                theta = omega * depth_step / velocity
                q = velocity / (omega * cell_width)
                spread = damping + 1j * paraxial_top * q / (1.0 + q)
                turn = np.exp(1j * theta)
                centre = turn * (1.0 - 4.0 * spread)
                beside = turn * spread
                table[j, :, s * per_chunk + i, :OUTSIDE] = np.stack(
                    [centre.real, centre.imag, beside.real, beside.imag]
                )
    return table.astype(np.float32)


def trace_basis(orders, nz, per_chunk, chunks):
    samples = 2 * orders
    times = np.arange(samples)[:, None] + 0.5
    order = [
        s * (orders // nz) + j * per_chunk + i
        for j in range(chunks)
        for s in range(nz)
        for i in range(per_chunk)
    ]
    angles = 2.0 * math.pi * (np.array(order)[None, :] + 1.0) * times / samples
    basis = np.concatenate([np.cos(angles), -np.sin(angles)], axis=1) / math.sqrt(orders)
    basis = basis.astype(np.float32)
    high = basis.astype(ml_dtypes.bfloat16)
    low = (basis - high.astype(np.float32)).astype(ml_dtypes.bfloat16)
    return np.concatenate([high, high, low], axis=1)


def predict_kernel(
    tiles, nz, per_chunk, chunks, rows, width,
    x_ref, strip_ref, level_ref, table_ref,
    m_ref, d_ref,
    ext, sext, lext, index, coef, state, other,
    a_send, a_recv, s_send, s_recv, r_send, r_recv, q_send, q_recv, l_send, l_recv, own,
):
    tile = lax.axis_index("tile")
    me = lax.axis_index("freq")
    has_up = tile > 0
    has_down = tile < tiles - 1
    nt = tile_count(width)
    mains = width // LANES
    full = rows + 2 * HALO
    inner = pl.ds(HALO, rows)
    window = pl.ds(pl.multiple_of(me * width, LANES), width + 2 * LANES)

    barrier = pltpu.get_barrier_semaphore()
    for hop in range(1, nz):
        pl.semaphore_signal(
            barrier, inc=1, device_id=(tile, lax.rem(me + hop, nz)), device_id_type=MESH
        )

    @pl.when(has_up)
    def _():
        pl.semaphore_signal(barrier, inc=1, device_id=(tile - 1, me), device_id_type=MESH)

    @pl.when(has_down)
    def _():
        pl.semaphore_signal(barrier, inc=1, device_id=(tile + 1, me), device_id_type=MESH)

    pl.semaphore_wait(
        barrier, nz - 1 + has_up.astype(jnp.int32) + has_down.astype(jnp.int32)
    )

    def level_copy(up):
        src = level_ref.at[pl.ds(0 if up else rows - HALO, HALO), window]
        dst = lext.at[pl.ds(HALO + rows if up else 0, HALO), :]
        way = 0 if up else 1
        return pltpu.make_async_remote_copy(
            src_ref=src, dst_ref=dst, send_sem=l_send.at[way], recv_sem=l_recv.at[way],
            device_id=(tile + (-1 if up else 1), me), device_id_type=MESH,
        )

    def main_copy(j, dest, source):
        return pltpu.make_async_remote_copy(
            src_ref=x_ref.at[
                :, pl.ds(j * per_chunk, per_chunk), :,
                pl.ds(pl.multiple_of(dest * width, LANES), width),
            ],
            dst_ref=ext.at[j, :, pl.ds(source * per_chunk, per_chunk), inner, :],
            send_sem=a_send.at[j, dest], recv_sem=a_recv.at[j, source],
            device_id=(tile, dest), device_id_type=MESH,
        )

    def strip_copy(j, dest, source):
        return pltpu.make_async_remote_copy(
            src_ref=strip_ref.at[dest, j],
            dst_ref=sext.at[j, source, inner, :],
            send_sem=s_send.at[j, dest], recv_sem=s_recv.at[j, source],
            device_id=(tile, dest), device_id_type=MESH,
        )

    def row_copies(j, up):
        src = pl.ds(HALO if up else rows, HALO)
        dst = pl.ds(HALO + rows if up else 0, HALO)
        way = 0 if up else 1
        target = (tile + (-1 if up else 1), me)
        return (
            pltpu.make_async_remote_copy(
                src_ref=ext.at[j, :, :, src, :], dst_ref=ext.at[j, :, :, dst, :],
                send_sem=r_send.at[j, way], recv_sem=r_recv.at[j, way],
                device_id=target, device_id_type=MESH,
            ),
            pltpu.make_async_remote_copy(
                src_ref=sext.at[j, :, src, :], dst_ref=sext.at[j, :, dst, :],
                send_sem=q_send.at[j, way], recv_sem=q_recv.at[j, way],
                device_id=target, device_id_type=MESH,
            ),
        )

    def own_copies(j):
        return (
            pltpu.make_async_copy(
                x_ref.at[
                    :, pl.ds(j * per_chunk, per_chunk), :,
                    pl.ds(pl.multiple_of(me * width, LANES), width),
                ],
                ext.at[j, :, pl.ds(me * per_chunk, per_chunk), inner, :],
                own.at[j, 0],
            ),
            pltpu.make_async_copy(
                strip_ref.at[me, j], sext.at[j, me, inner, :], own.at[j, 1]
            ),
        )

    own_level = pltpu.make_async_copy(
        level_ref.at[:, window], lext.at[inner, :], own.at[chunks, 0]
    )

    @pl.when(has_up)
    def _():
        level_copy(True).start()

    @pl.when(has_down)
    def _():
        level_copy(False).start()

    own_level.start()

    def send(j):
        for hop in range(1, nz):
            dest = lax.rem(me + hop, nz)
            strip_copy(j, dest, me).start()
            main_copy(j, dest, me).start()

    def sent(j):
        for hop in range(1, nz):
            dest = lax.rem(me + hop, nz)
            strip_copy(j, dest, me).wait_send()
            main_copy(j, dest, me).wait_send()

    send(0)

    def keep(j, carry):
        for copy in own_copies(j):
            copy.start()
        return carry

    lax.fori_loop(0, chunks, keep, 0)

    top, bottom = pl.ds(0, HALO), pl.ds(HALO + rows, HALO)
    for missing, edge in ((jnp.logical_not(has_up), top), (jnp.logical_not(has_down), bottom)):

        @pl.when(missing)
        def _(edge=edge):
            lext[edge, :] = jnp.full((HALO, lext.shape[1]), OUTSIDE, jnp.int32)

            def clear(j, carry):
                for part in range(2):
                    for f in range(8):
                        ext[j, part, f, edge, :] = jnp.zeros((HALO, width), jnp.float32)
                for s in range(nz):
                    sext[j, s, edge, :] = jnp.zeros((HALO, LANES), jnp.float32)
                return carry

            lax.fori_loop(0, chunks, clear, 0)

    own_level.wait()

    @pl.when(has_up)
    def _():
        level_copy(True).wait_send()
        level_copy(False).wait_recv()

    @pl.when(has_down)
    def _():
        level_copy(False).wait_send()
        level_copy(True).wait_recv()

    lane2 = lax.broadcasted_iota(jnp.int32, (8, LANES), 1)
    lane3 = lax.broadcasted_iota(jnp.int32, (8, 8, LANES), 2)

    def make_index(b, carry):
        at = pl.ds(pl.multiple_of(b * 8, 8), 8)
        pieces = [lext[at, k * LANES : (k + 1) * LANES] for k in range(mains + 2)]
        for t in range(nt):
            found = overlapped(pieces, t, lane2)
            index[t, at] = jnp.broadcast_to(found[:, None, :], (8, 8, LANES))
        return carry

    lax.fori_loop(0, full // 8, make_index, 0)

    def arrive(j):
        sent(j)

        @pl.when(j + 1 < chunks)
        def _():
            send(j + 1)

        for copy in own_copies(j):
            copy.wait()
        for hop in range(1, nz):
            source = lax.rem(me + hop, nz)
            main_copy(j, me, source).wait_recv()
            strip_copy(j, me, source).wait_recv()

        @pl.when(has_up)
        def _():
            for copy in row_copies(j, True):
                copy.start()

        @pl.when(has_down)
        def _():
            for copy in row_copies(j, False):
                copy.start()

    arrive(0)

    def one_chunk(j, carry):
        def make_coef(b, carry):
            values = [table_ref[j, c] for c in range(4)]
            for r in range(8):
                for t in range(nt):
                    at = index[t, 8 * b + r]
                    for c in range(4):
                        coef[c, t, 8 * b + r] = jnp.take_along_axis(
                            values[c], at, axis=1, mode="promise_in_bounds"
                        )
            return carry

        lax.fori_loop(0, full // 8, make_coef, 0)

        @pl.when(has_up)
        def _():
            for copy in row_copies(j, False):
                copy.wait_recv()

        @pl.when(has_down)
        def _():
            for copy in row_copies(j, True):
                copy.wait_recv()

        def fill(b, carry):
            at = pl.ds(pl.multiple_of(b * 8, 8), 8)
            for part in range(2):
                main = [
                    jnp.swapaxes(ext[j, part, :, at, k * LANES : (k + 1) * LANES], 0, 1)
                    for k in range(mains)
                ]
                strips = []
                for s in range(nz):
                    strip = sext[j, s, at, :]
                    for i in range(per_chunk):
                        base = (part * per_chunk + i) * 2 * HALO
                        strips.append(pltpu.roll(strip, (LANES - base - HALO) % LANES, 1))
                strip = jnp.swapaxes(jnp.stack(strips), 0, 1)
                pieces = [strip] + main + [strip]
                for t in range(nt):
                    state[part, t, at] = overlapped(pieces, t, lane3)

                @pl.when((b >= HALO // 8) & (b < (HALO + rows) // 8))
                def _():
                    for k in range(mains):
                        for r in range(8):
                            d_ref[b * 8 - HALO + r, k, part, j] = main[k][r]
            return carry

        lax.fori_loop(0, full // 8, fill, 0)

        def one_step(s, old, new):
            first = HALO - filter_reach - STEPS + s
            count = rows + 2 * (filter_reach + STEPS) - 2 * s

            def block(b, carry):
                e = first + ROWS * b

                def row(r):
                    return [(old[0, t, e + r], old[1, t, e + r]) for t in range(nt)]

                above, here = row(-1), row(0)
                for r in range(ROWS):
                    below = row(r + 1)
                    for t in range(nt):
                        p, q = here[t]
                        nr = (above[t][0] + below[t][0]) + (
                            pltpu.roll(p, 1, 1) + pltpu.roll(p, LANES - 1, 1)
                        )
                        ni = (above[t][1] + below[t][1]) + (
                            pltpu.roll(q, 1, 1) + pltpu.roll(q, LANES - 1, 1)
                        )
                        cr, ci = coef[0, t, e + r], coef[1, t, e + r]
                        br, bi = coef[2, t, e + r], coef[3, t, e + r]
                        new[0, t, e + r] = (cr * p - ci * q) + (br * nr - bi * ni)
                        new[1, t, e + r] = (cr * q + ci * p) + (br * ni + bi * nr)
                    above, here = here, below
                return carry

            lax.fori_loop(0, (count + ROWS - 1) // ROWS, block, 0)

        def two_steps(n, carry):
            @pl.when((n == STEPS // 2 - 1) & (j + 1 < chunks))
            def _():
                arrive(j + 1)

            one_step(2 * n + 1, state, other)
            one_step(2 * n + 2, other, state)
            return carry

        lax.fori_loop(0, STEPS // 2, two_steps, 0)

        def put(b, carry):
            for r in range(4):
                for t in range(nt):
                    for part in range(2):
                        m_ref[4 * b + r, t, part, j] = state[
                            part, t, 4 * b + r + HALO - filter_reach
                        ]
            return carry

        lax.fori_loop(0, (rows + 8) // 4, put, 0)
        return carry

    lax.fori_loop(0, chunks, one_chunk, 0)

    def finish(j, carry):
        @pl.when(has_up)
        def _():
            for copy in row_copies(j, True):
                copy.wait_send()

        @pl.when(has_down)
        def _():
            for copy in row_copies(j, False):
                copy.wait_send()

        return carry

    lax.fori_loop(0, chunks, finish, 0)


def to_trace(basis, spectrum):
    high = spectrum.astype(jnp.bfloat16)
    low = (spectrum - high.astype(jnp.float32)).astype(jnp.bfloat16)
    both = jnp.concatenate([high, low, high], axis=0)
    return jnp.dot(basis, both, preferred_element_type=jnp.float32)


def subtract_kernel(
    rows, width, m_ref, d_ref, basis_ref, p_ref, q_ref, shifted, power, data, result
):
    i = pl.program_id(0)
    mains = width // LANES
    nt = m_ref.shape[1]
    reach = filter_reach
    diameter = 2 * reach + 1
    samples = basis_ref.shape[0]
    basis = basis_ref[...]
    lane = lax.broadcasted_iota(jnp.int32, (samples, LANES), 1)

    def traces(ref, first, count):
        spectrum = jnp.concatenate(
            [
                ref[first + r, t].reshape(samples, LANES)
                for r in range(TOGETHER)
                for t in range(count)
            ],
            axis=1,
        )
        found = to_trace(basis, spectrum)
        return [
            [
                found[:, (r * count + t) * LANES : (r * count + t + 1) * LANES]
                for t in range(count)
            ]
            for r in range(TOGETHER)
        ]

    def make_rows(n, carry):
        for r, tiles in enumerate(traces(m_ref, TOGETHER * n, nt)):
            row = TOGETHER * n + r
            for b in range(mains):
                total = None
                for shift in range(diameter):
                    low = LANES * b + shift - reach
                    value = None
                    for t in range(nt):
                        begin, end = STRIDE * t - reach, STRIDE * (t + 1) - reach
                        if end <= low or begin >= low + LANES:
                            continue
                        turn = (STRIDE * t - HALO - low) % LANES
                        moved = pltpu.roll(tiles[t], turn, 1) if turn else tiles[t]
                        value = (
                            moved
                            if value is None
                            else jnp.where(lane < begin - low, value, moved)
                        )
                    value = -value
                    shifted[shift, b, row] = value
                    part = jnp.sum((value * value).reshape(samples // 8, 8, LANES), axis=0)
                    total = part if total is None else total + part
                power[b, row] = total
        return carry

    lax.fori_loop(
        jnp.where(i == 0, 0, (8 * i + 2 * reach) // TOGETHER),
        (8 * i + 8 + 2 * reach) // TOGETHER,
        make_rows,
        0,
    )

    def make_data(n, carry):
        for r, tiles in enumerate(traces(d_ref, 8 * i + TOGETHER * n, mains)):
            for b in range(mains):
                data[b, TOGETHER * n + r] = tiles[b]
        return carry

    lax.fori_loop(0, 8 // TOGETHER, make_data, 0)

    taps = [(a, c) for a in range(diameter) for c in range(diameter)]

    def total(values):
        return jnp.sum(values, axis=0, keepdims=True)

    def one_row(r, carry):
        for b in range(mains):
            one_tile(r, b)
        return carry

    def one_tile(r, b):
        def tap(a, c):
            return shifted[c, b, 8 * i + r + a]

        recorded = data[b, r]
        energy = power[b, 8 * i + r]
        for a in range(1, diameter):
            energy = energy + power[b, 8 * i + r + a]
        gain = step_size / (energy_floor + total(energy))

        def remove(weights):
            residual = recorded
            for weight, (a, c) in zip(weights, taps):
                residual = residual - weight * tap(a, c)
            return residual

        weights = [total(recorded * tap(a, c)) * gain for a, c in taps]
        for repeat in range(1, PASSES):
            residual = remove(weights)
            weights = [
                w + total(residual * tap(a, c)) * gain for w, (a, c) in zip(weights, taps)
            ]
        result[b, r] = remove(weights)

    lax.fori_loop(0, 8, one_row, 0)

    for b in range(mains):
        at = slice(b * LANES, (b + 1) * LANES)
        for k in range(samples // 8):
            part = slice(8 * k, 8 * k + 8)
            p_ref[part, :, at] = jnp.swapaxes(result[b, :, part, :], 0, 1)
            q_ref[part, :, at] = jnp.swapaxes(
                shifted[reach, b, pl.ds(8 * i + reach, 8), part, :], 0, 1
            )


def local(mesh_shape, data_spectrum, velocity_level):
    nz, tiles = mesh_shape["freq"], mesh_shape["tile"]
    _, local_freqs, rows, cols = data_spectrum.shape
    orders = local_freqs * nz
    samples = 2 * orders
    width = cols // nz
    per_chunk = 8 // nz
    chunks = local_freqs // per_chunk
    nt = tile_count(width)
    mains = width // LANES
    full = rows + 2 * HALO
    reach = filter_reach

    around = jnp.pad(data_spectrum, ((0, 0), (0, 0), (0, 0), (HALO, HALO)))
    strips = jnp.stack(
        [
            jnp.concatenate(
                [
                    around[..., d * width : d * width + HALO],
                    around[..., (d + 1) * width + HALO : (d + 1) * width + 2 * HALO],
                ],
                axis=-1,
            )
            for d in range(nz)
        ]
    )
    strips = strips.reshape(nz, 2, chunks, per_chunk, rows, 2 * HALO)
    strips = strips.transpose(0, 2, 4, 1, 3, 5).reshape(nz, chunks, rows, -1)
    strips = jnp.pad(strips, ((0, 0),) * 3 + ((0, LANES - strips.shape[-1]),))
    levels = jnp.pad(velocity_level, ((0, 0), (LANES, LANES)), constant_values=OUTSIDE)
    table = jnp.asarray(coefficient_table(orders, nz, per_chunk, chunks))
    basis = jnp.asarray(trace_basis(orders, nz, per_chunk, chunks))

    dma = pltpu.SemaphoreType.DMA
    vmem = pl.BlockSpec(memory_space=pltpu.VMEM)
    hbm = pl.BlockSpec(memory_space=pl.ANY)
    predicted, recorded = pl.pallas_call(
        functools.partial(predict_kernel, tiles, nz, per_chunk, chunks, rows, width),
        out_shape=(
            jax.ShapeDtypeStruct((rows + 8, nt, 2, chunks, 8, LANES), jnp.float32),
            jax.ShapeDtypeStruct((rows, mains, 2, chunks, 8, LANES), jnp.float32),
        ),
        in_specs=[hbm, hbm, hbm, vmem],
        out_specs=(vmem, vmem),
        scratch_shapes=[
            pltpu.VMEM((chunks, 2, 8, full, width), jnp.float32),
            pltpu.VMEM((chunks, nz, full, LANES), jnp.float32),
            pltpu.VMEM((full, width + 2 * LANES), jnp.int32),
            pltpu.VMEM((nt, full, 8, LANES), jnp.int32),
            pltpu.VMEM((4, nt, full + ROWS, 8, LANES), jnp.float32),
            pltpu.VMEM((2, nt, full + ROWS, 8, LANES), jnp.float32),
            pltpu.VMEM((2, nt, full + ROWS, 8, LANES), jnp.float32),
            dma((chunks, nz)), dma((chunks, nz)), dma((chunks, nz)), dma((chunks, nz)),
            dma((chunks, 2)), dma((chunks, 2)), dma((chunks, 2)), dma((chunks, 2)),
            dma((2,)), dma((2,)), dma((chunks + 1, 2)),
        ],
        compiler_params=pltpu.CompilerParams(
            collective_id=0, has_side_effects=True, vmem_limit_bytes=56 * 2**20
        ),
        name="predict",
    )(data_spectrum, strips, levels, table)

    block = pl.BlockSpec((samples, 8, width), lambda i: (0, i, 0))
    out = jax.ShapeDtypeStruct((samples, rows, width), jnp.float32)
    return pl.pallas_call(
        functools.partial(subtract_kernel, rows, width),
        grid=(rows // 8,),
        out_shape=(out, out),
        in_specs=[vmem, vmem, vmem],
        out_specs=(block, block),
        scratch_shapes=[
            pltpu.VMEM((2 * reach + 1, mains, rows + 2 * reach, samples, LANES), jnp.float32),
            pltpu.VMEM((mains, rows + 2 * reach, 8, LANES), jnp.float32),
            pltpu.VMEM((mains, 8, samples, LANES), jnp.float32),
            pltpu.VMEM((mains, 8, samples, LANES), jnp.float32),
        ],
        compiler_params=pltpu.CompilerParams(vmem_limit_bytes=56 * 2**20),
        name="subtract",
    )(predicted, recorded, basis)


def solution(mesh):
    in_specs = (P(None, "freq", "tile", None), P("tile", None))
    out_specs = (P(None, "tile", "freq"), P(None, "tile", "freq"))
    return jax.shard_map(
        functools.partial(local, dict(mesh.shape)),
        mesh=mesh, in_specs=in_specs, out_specs=out_specs, check_vma=False,
    )
```
